32 devices in a mesh: fsdp: 16 (over z, x, core), expert: 2 (over y).
Axes of the slice: x: 2, y: 2, z: 4, core: 2. Of those that a mesh axis runs over, the one named last changes fastest.
Arguments:
- prompt_in: bfloat16 [16, 1024, 768], P('fsdp', 'expert'), may hold values from -6 to 6
- cont_in: bfloat16 [16, 2, 512, 768], P('fsdp', 'expert'), may hold values from -6 to 6
- prompt_cot: bfloat16 [16, 1024, 768], P('fsdp', 'expert'), may hold values from -6 to 6
- cont_cot: bfloat16 [16, 2, 512, 768], P('fsdp', 'expert'), may hold values from -6 to 6
- prompt_route: int32 [16, 1024, 2], P('fsdp', 'expert'), may hold values from 0 to 7, all different within a row
- cont_route: int32 [16, 2, 512, 2], P('fsdp', 'expert'), may hold values from 0 to 7, all different within a row
- rel_bucket: int32 [1536], replicated, may hold values from 0 to 31
- norm_attn: bfloat16 [768], P('fsdp'), may hold values from 0.25 to 1.75
- norm_ffn: bfloat16 [768], P('fsdp'), may hold values from 0.25 to 1.75
- w_qkv: bfloat16 [768, 2304], P('fsdp'), may hold values from -0.21875 to 0.21875
- w_out: bfloat16 [768, 768], P('fsdp'), may hold values from -0.875 to 0.875
- rel_w: bfloat16 [32, 12], P('fsdp'), may hold values from -4 to 4
- w_router: bfloat16 [768, 8], P('fsdp'), may hold values from -0.14941406 to 0.14941406
- expert_in: bfloat16 [8, 768, 3072], P('expert', 'fsdp'), may hold values from -0.21875 to 0.21875
- expert_out: bfloat16 [8, 3072, 768], P('expert', 'fsdp'), may hold values from -0.15625 to 0.15625
Outputs:
- prompt_out: bfloat16 [16, 1024, 768], P('fsdp', 'expert')
- cont_out: bfloat16 [16, 2, 512, 768], P('fsdp', 'expert')
- prompt_grad: float32 [16, 1024, 768], P('fsdp', 'expert')
- cont_grad: float32 [16, 2, 512, 768], P('fsdp', 'expert')
- grad_norm_attn: float32 [768], P('fsdp')
- grad_norm_ffn: float32 [768], P('fsdp')
- grad_qkv: float32 [768, 2304], P('fsdp')
- grad_out: float32 [768, 768], P('fsdp')
- grad_rel: float32 [32, 12], P('fsdp')
- grad_router: float32 [768, 8], P('fsdp')
- grad_expert_in: float32 [8, 768, 3072], P('expert', 'fsdp')
- grad_expert_out: float32 [8, 3072, 768], P('expert', 'fsdp')
The draws below stay inside these ranges and needn't reach their ends.
Inputs may be any that keep to these rules, and one draw needn't show every extreme that they name: `prompt_route`: each row names two different experts. `cont_route`: each row names two different experts.
All inputs are finite; a program needn't handle non-finite values.
Results may differ from the reference program's by a relative error of at most 0.03.
Values may be sent and summed in bfloat16 or wider, within the bound.
A program may use at most 512 MiB of HBM per device.

```python
import jax
import jax.numpy as jnp
from jax import lax

D = 768
HEADS = 12
HEAD_DIM = 64
FF = 3072
NB = 32
CLEN = 512
PROMPT = 1024
GROUPS = 16
CONTS = 2
PROMPT_DEV = 512
EXPERTS = 8
CAP_P = 160
CAP_C = 160
DIST = 1536
N_EXPERT = 2


def plant(values, rng, low, high):
    extent = values.shape
    spot = [jax.random.randint(jax.random.fold_in(rng, axis), (), 0, extent[axis]) for axis in range(len(extent))]
    values = values.at[tuple(spot)].set(low)
    longest = extent.index(max(extent))
    spot[longest] = (spot[longest] + 1) % extent[longest]
    return values.at[tuple(spot)].set(high)


def levels(key, shape, cuts, smallest, top_value):
    def one(dim, shards_of):
        heights = jax.random.uniform(jax.random.fold_in(jax.random.fold_in(key, 6), dim), (shards_of,), jnp.float32, smallest / len(cuts), top_value / len(cuts))
        return jnp.repeat(jnp.exp(heights), shape[dim] // shards_of).reshape((-1,) + (1,) * (len(shape) - dim - 1))

    level = one(*cuts[0])
    for cut in cuts[1:]:
        level = level * one(*cut)
    return level


def distinct(rng, rows, amount, top, lift):
    sequence = jax.random.permutation(jax.random.fold_in(rng, 1), amount)
    pull = sequence
    for power in range(3):
        pull = pull * pull // amount
    pull = pull * lift // amount
    chance = jax.random.randint(jax.random.fold_in(rng, 2), (rows, amount), 0, 4096) + pull
    holders = jax.random.permutation(jax.random.fold_in(rng, 3), rows)[jnp.arange(amount) % rows]
    chance = jnp.where(jnp.arange(rows)[:, None] == holders[None, :], 1 << 14, chance)
    priority = chance * amount + jnp.arange(amount)
    return lax.top_k(priority.astype(jnp.int32), top)[1].astype(jnp.int32)


def bell_draw(stream_key, dims, width, bound, shards=(), kind=jnp.bfloat16):
    entries = width * jax.random.normal(stream_key, dims, jnp.float32)
    if shards:
        entries = entries * levels(stream_key, dims, shards, -0.22, 0.18)
    return jnp.clip(entries, -bound, bound).astype(kind)


def setup_inputs(seed: int = 0) -> dict:
    key_of = jax.random.split(jax.random.key(seed), 16)
    prompt_in = bell_draw(key_of[0], (GROUPS, PROMPT, D), 1.0, 6.0, ((0, 16), (1, 2)))
    cont_in = bell_draw(key_of[1], (GROUPS, CONTS, CLEN, D), 1.0, 6.0, ((0, 16), (1, 2)))
    prompt_cot = bell_draw(key_of[2], (GROUPS, PROMPT, D), 1.0, 6.0, ((0, 16), (1, 2)))
    cont_cot = bell_draw(key_of[3], (GROUPS, CONTS, CLEN, D), 1.0, 6.0, ((0, 16), (1, 2)))
    prompt_route = distinct(key_of[4], GROUPS * PROMPT, EXPERTS, 2, 2048).reshape((GROUPS, PROMPT, 2))
    cont_route = distinct(key_of[5], GROUPS * CONTS * CLEN, EXPERTS, 2, 2048).reshape((GROUPS, CONTS, CLEN, 2))
    rel_bucket = plant(jax.random.randint(key_of[6], (DIST,), 0, NB), jax.random.fold_in(key_of[6], 1), 0, NB - 1).astype(jnp.int32)
    norm_attn = jnp.clip(1.0 + 0.15 * jax.random.normal(key_of[7], (D,), jnp.float32), 0.25, 1.75).astype(jnp.bfloat16)
    norm_ffn = jnp.clip(1.0 + 0.15 * jax.random.normal(key_of[8], (D,), jnp.float32), 0.25, 1.75).astype(jnp.bfloat16)
    w_qkv = bell_draw(key_of[9], (D, 3 * D), D ** -0.5, 0.21875, ((0, 16),))
    w_out = bell_draw(key_of[10], (D, D), (D // 16) ** -0.5, 0.875, ((0, 16),))
    rel_w = bell_draw(key_of[11], (NB, HEADS), 1.0, 4.0, ((0, 16),))
    w_router = bell_draw(key_of[12], (D, EXPERTS), 0.025, 0.14941406, ((0, 16),))
    expert_in = bell_draw(key_of[13], (EXPERTS, D, FF), D ** -0.5, 0.21875, ((0, 2), (1, 16)))
    expert_out = bell_draw(key_of[14], (EXPERTS, FF, D), (FF // 2) ** -0.5, 0.15625, ((0, 2), (1, 16)))
    return dict(prompt_in=prompt_in, cont_in=cont_in, prompt_cot=prompt_cot, cont_cot=cont_cot, prompt_route=prompt_route, cont_route=cont_route, rel_bucket=rel_bucket, norm_attn=norm_attn, norm_ffn=norm_ffn, w_qkv=w_qkv, w_out=w_out, rel_w=rel_w, w_router=w_router, expert_in=expert_in, expert_out=expert_out)


epsilon = 1e-06
blocked = -1e+30
highest = lax.Precision.HIGHEST

@jax.custom_vjp
def low(v):
    return lax.optimization_barrier(v.astype(jnp.bfloat16)).astype(jnp.float32)

@jax.custom_vjp
def low_back(v):
    return v

def low_keep(v):
    return (low(v), None)

def low_pass(kept, grad):
    return (grad,)

def back_keep(v):
    return (v, None)

def back_low(kept, grad):
    return (low(grad),)
low.defvjp(low_keep, low_pass)
low_back.defvjp(back_keep, back_low)

def matmul_high(left, right):
    return jnp.dot(left, right, precision=highest, preferred_element_type=jnp.float32)

def rms_scale(inputs, gain):
    return inputs * lax.rsqrt(lax.optimization_barrier(jnp.mean(inputs * inputs, axis=-1, keepdims=True)) + epsilon) * gain

def gate_weights(logits, routes):
    probs = jax.nn.softmax(logits, axis=-1)
    picked = jnp.take_along_axis(probs, routes, axis=-1)
    return picked / lax.optimization_barrier(jnp.sum(picked, axis=-1, keepdims=True))

def slot_positions(routes, experts, capacity):
    flat_ids = routes.reshape(-1)
    one_hot = (flat_ids[:, None] == jnp.arange(experts, dtype=jnp.int32)[None, :]).astype(jnp.int32)
    earlier = jnp.cumsum(one_hot, axis=0) - one_hot
    slot_num = lax.optimization_barrier(jnp.sum(earlier * one_hot, axis=1))
    placed = jnp.where(slot_num < capacity, flat_ids * capacity + slot_num, -1)
    return placed.reshape(routes.shape).astype(jnp.int32)

def attend(query, key_rows, value_rows, query_pos, key_pos, dist_table):
    distance = query_pos[:, None] - key_pos[None, :]
    rel_bias = jnp.take(dist_table, jnp.maximum(distance, 0), axis=1)
    logit_raw = jnp.einsum('qhd,khd->hqk', query, key_rows, precision=highest) * query.shape[-1] ** (-0.5) + rel_bias
    scores = jnp.where(distance[None] >= 0, low_back(logit_raw), blocked)
    probs = low(jax.nn.softmax(scores, axis=-1))
    return jnp.einsum('hqk,khd->qhd', probs, value_rows, precision=highest)

def mixture(unit_rows, placed, gate_vals, capacity, w_in, w_down):
    sources = unit_rows.shape[0]
    slot_ids = jnp.arange(EXPERTS * capacity, dtype=jnp.int32)
    dispatch_table = jnp.any(placed[..., None] == slot_ids, axis=2).astype(jnp.float32)
    outbound = low_back(jnp.einsum('srn,srd->snd', dispatch_table, unit_rows, precision=highest))
    outbound = outbound.reshape(sources, EXPERTS, capacity, D)
    before = low_back(jnp.einsum('secd,edf->secf', outbound, w_in, precision=highest))
    active = low(jax.nn.gelu(before))
    produced = low(low_back(jnp.einsum('secf,efd->secd', active, w_down, precision=highest)))
    flat_out = produced.reshape(sources, EXPERTS * capacity, D)
    is_valid = placed >= 0
    picked = jax.vmap(lambda table_rows, index_rows: jnp.take(table_rows, index_rows, axis=0))(flat_out, jnp.maximum(placed, 0))
    return lax.optimization_barrier(jnp.sum(jnp.where(is_valid, gate_vals, 0.0)[..., None] * picked, axis=2))

def block_forward(prompt_x, cont_x, gain_attn, gain_ffn, w_qkv, w_out, rel_w, w_router, w_in, w_down, place_prompt, place_cont, route_prompt, route_cont, rel_bucket):
    every_row = jnp.concatenate([prompt_x, cont_x.reshape(-1, D)], axis=0)
    normed = low(rms_scale(every_row, gain_attn))
    joined = low_back(matmul_high(normed, w_qkv))
    query = low(joined[:, :D]).reshape(-1, HEADS, HEAD_DIM)
    key_rows = low(joined[:, D:2 * D]).reshape(-1, HEADS, HEAD_DIM)
    value_rows = low(joined[:, 2 * D:]).reshape(-1, HEADS, HEAD_DIM)
    dist_table = jnp.take(rel_w, rel_bucket, axis=0).T
    prompt_pos = jnp.arange(PROMPT, dtype=jnp.int32)
    cont_pos = PROMPT + jnp.arange(CLEN, dtype=jnp.int32)
    attn_prompt = attend(query[:PROMPT], key_rows[:PROMPT], value_rows[:PROMPT], prompt_pos, prompt_pos, dist_table)

    def one_cont(cont_query, cont_keys, cont_values):
        return attend(cont_query, jnp.concatenate([key_rows[:PROMPT], cont_keys]), jnp.concatenate([value_rows[:PROMPT], cont_values]), cont_pos, jnp.concatenate([prompt_pos, cont_pos]), dist_table)
    shaped = (CONTS, CLEN, HEADS, HEAD_DIM)
    attn_cont = jax.vmap(one_cont)(query[PROMPT:].reshape(shaped), key_rows[PROMPT:].reshape(shaped), value_rows[PROMPT:].reshape(shaped))
    heads_out = jnp.concatenate([attn_prompt.reshape(-1, D), attn_cont.reshape(-1, D)], axis=0)
    heads_out = low(low_back(heads_out))
    middle = every_row + low_back(matmul_high(heads_out, w_out))
    normed_ffn = low(rms_scale(middle, gain_ffn))
    logits = matmul_high(normed_ffn, w_router)
    all_routes = jnp.concatenate([route_prompt, route_cont.reshape(-1, 2)], axis=0)
    gate_vals = gate_weights(logits, all_routes)
    moe_prompt = mixture(normed_ffn[:PROMPT].reshape(N_EXPERT, PROMPT_DEV, D), place_prompt, gate_vals[:PROMPT].reshape(N_EXPERT, PROMPT_DEV, 2), CAP_P, w_in, w_down)
    moe_cont = mixture(normed_ffn[PROMPT:].reshape(CONTS, CLEN, D), place_cont, gate_vals[PROMPT:].reshape(CONTS, CLEN, 2), CAP_C, w_in, w_down)
    mixed_out = middle + jnp.concatenate([moe_prompt.reshape(-1, D), moe_cont.reshape(-1, D)], axis=0)
    return (mixed_out[:PROMPT], mixed_out[PROMPT:].reshape(CONTS, CLEN, D))

def reference(prompt_in, cont_in, prompt_cot, cont_cot, prompt_route, cont_route, rel_bucket, norm_attn, norm_ffn, w_qkv, w_out, rel_w, w_router, expert_in, expert_out):
    weights = tuple((array.astype(jnp.float32) for array in (norm_attn, norm_ffn, w_qkv, w_out, rel_w, w_router, expert_in, expert_out)))

    def one_group(totals, group_item):
        prompt_x, cont_x, prompt_c, cont_c, route_p, route_c = group_item
        place_prompt = jax.vmap(lambda rows: slot_positions(rows, EXPERTS, CAP_P))(route_p.reshape(N_EXPERT, PROMPT_DEV, 2))
        place_cont = jax.vmap(lambda rows: slot_positions(rows, EXPERTS, CAP_C))(route_c)

        def run_block(*values):
            return block_forward(*values, place_prompt, place_cont, route_p, route_c, rel_bucket)
        results, pullback = jax.vjp(run_block, prompt_x.astype(jnp.float32), cont_x.astype(jnp.float32), *weights)
        gradients = pullback((prompt_c.astype(jnp.float32), cont_c.astype(jnp.float32)))
        totals = tuple((total + grad for total, grad in zip(totals, gradients[2:])))
        return (totals, (results[0].astype(jnp.bfloat16), results[1].astype(jnp.bfloat16), gradients[0], gradients[1]))
    zero_grads = tuple((jnp.zeros(array.shape, jnp.float32) for array in weights))
    totals, stacked = lax.scan(one_group, zero_grads, (prompt_in, cont_in, prompt_cot, cont_cot, prompt_route, cont_route))
    return (stacked[0], stacked[1], stacked[2], stacked[3], totals[0], totals[1], totals[2], totals[3], totals[4], totals[5], totals[6], totals[7])
```

```python
import functools

import jax
import jax.numpy as jnp
from jax import lax
from jax.experimental import pallas as pl
from jax.experimental.pallas import tpu as pltpu
from jax.sharding import PartitionSpec as P

epsilon = 1e-06
blocked = -1e30
f32 = jnp.float32
bf16 = jnp.bfloat16
KB = 128
VMEM_LIMIT = 60 * 1024 * 1024


def nn(a, b):
    return lax.dot_general(a, b, (((1,), (0,)), ((), ())), preferred_element_type=f32)


def nt(a, b):
    return lax.dot_general(a, b, (((1,), (1,)), ((), ())), preferred_element_type=f32)


def tn(a, b):
    return lax.dot_general(a, b, (((0,), (0,)), ((), ())), preferred_element_type=f32)


def make_strips(table_ref, strip_ref):
    width = strip_ref.shape[2]
    for h in range(2):
        wide = jnp.broadcast_to(table_ref[0, h : h + 1, :], (KB, width))
        strip_ref[h] = pltpu.roll(wide, 0, 1, stride=1, stride_axis=0)


def query_sets(own, n_prompt, n_cont, group, most):
    prompt_len = group * n_prompt
    rows = n_prompt + n_cont
    place = [lax.rem(own + s, group) * n_prompt for s in range(group)]
    start = [0] + [rows + s * n_prompt for s in range(group - 1)]
    sets = []
    for base, count, first_place in ((0, n_prompt, place[0]), (n_prompt, n_cont, prompt_len)):
        size = most if count % most == 0 else count
        for first in range(0, count, size):
            keys = [(base, first + size, prompt_len + first)]
            for s in range(group):
                if base or s:
                    keys.append((start[s], n_prompt, prompt_len + first_place + first - place[s]))
            sets.append((base + first, size, keys))
    return sets


def strip_window(strip_ref, h, offset, keys, rows):
    parts = []
    for kb in range(keys // KB):
        start = offset - kb * KB
        if not isinstance(start, int):
            start = pl.multiple_of(start, KB)
        parts.append(strip_ref[h, :, pl.ds(start, rows)])
    return parts[0] if len(parts) == 1 else jnp.concatenate(parts, axis=0)


def head_lanes(x, h, head_size):
    lanes = lax.broadcasted_iota(jnp.int32, x.shape, 1)
    return jnp.where((lanes >= h * head_size) & (lanes < (h + 1) * head_size), x, jnp.zeros_like(x))


def attend_kernel(n_prompt, n_cont, group, head_size, own_ref, table_ref, q_ref, k_ref, v_ref, o_ref, lse_ref, strip_ref):
    make_strips(table_ref, strip_ref)
    scale = jnp.asarray(head_size**-0.5, bf16)
    for first, rows, keys in query_sets(own_ref[0], n_prompt, n_cont, group, 512):
        q_pair = q_ref[first : first + rows, :] * scale
        heads = []
        for h in range(2):
            q = head_lanes(q_pair, h, head_size)
            m = l = acc = None
            for start, count, offset in keys:
                s = nt(k_ref[start : start + count, :], q) + strip_window(strip_ref, h, offset, count, rows)
                top = jnp.max(s, axis=0, keepdims=True)
                m_new = top if m is None else jnp.maximum(m, top)
                p = jnp.exp(s - m_new)
                total = jnp.sum(p, axis=0, keepdims=True)
                out = tn(v_ref[start : start + count, :], p.astype(bf16))[h * head_size : (h + 1) * head_size]
                if m is None:
                    l, acc = total, out
                else:
                    shrink = jnp.exp(m - m_new)
                    l, acc = l * shrink + total, acc * shrink + out
                m = m_new
            heads.append(acc / l)
            lse_ref[0, h : h + 1, first : first + rows] = m + jnp.log(l)
        o_ref[first : first + rows, :] = jnp.concatenate(heads, axis=0).T.astype(bf16)


def attend_grad_kernel(n_prompt, n_cont, group, head_size, own_ref, table_ref, q_ref, k_ref, v_ref, o_ref, do_ref, lse_ref,
                       dqkv_ref, drel_ref, strip_ref, diag_ref, dk_ref, dv_ref):
    make_strips(table_ref, strip_ref)
    width = strip_ref.shape[2]
    mine = n_prompt + n_cont
    scale = jnp.asarray(head_size**-0.5, bf16)
    diag_ref[...] = jnp.zeros_like(diag_ref)
    dk_ref[...] = jnp.zeros_like(dk_ref)
    dv_ref[...] = jnp.zeros_like(dv_ref)
    for first, rows, keys in query_sets(own_ref[0], n_prompt, n_cont, group, 256):
        q_pair = q_ref[first : first + rows, :] * scale
        do_pair = do_ref[first : first + rows, :]
        inner = (do_pair.astype(f32) * o_ref[first : first + rows, :].astype(f32)).T
        heads = []
        for h in range(2):
            q = head_lanes(q_pair, h, head_size)
            do = head_lanes(do_pair, h, head_size)
            delta = jnp.sum(inner[h * head_size : (h + 1) * head_size], axis=0, keepdims=True)
            lse = lse_ref[0, h : h + 1, first : first + rows]
            dq = None
            for start, count, offset in keys:
                at = slice(start, start + count)
                k = k_ref[at, :]
                s = nt(k, q) + strip_window(strip_ref, h, offset, count, rows)
                p = jnp.exp(s - lse)
                ds = p * (nt(v_ref[at, :], do) - delta)
                for kb in range(count // KB):
                    lane = offset - kb * KB
                    if not isinstance(lane, int):
                        lane = pl.multiple_of(lane, KB)
                    diag_ref[h, :, pl.ds(lane, rows)] += ds[kb * KB : (kb + 1) * KB]
                ds = ds.astype(bf16)
                dv_ref[at, :] += nn(p.astype(bf16), do)
                dk_ref[at, :] += nn(ds, q)
                part = tn(k, ds)[h * head_size : (h + 1) * head_size]
                dq = part if dq is None else dq + part
            heads.append(dq)
        dqkv_ref[0, first : first + rows, :] = (jnp.concatenate(heads, axis=0).T * (head_size**-0.5)).astype(bf16)
    if dqkv_ref.shape[1] > mine:
        dqkv_ref[0, mine:, :] = jnp.zeros((dqkv_ref.shape[1] - mine, dqkv_ref.shape[2]), bf16)
    dqkv_ref[1] = dk_ref[...].astype(bf16)
    dqkv_ref[2] = dv_ref[...].astype(bf16)
    for h in range(2):
        x = diag_ref[h]
        half = KB // 2
        while half >= 8:
            x = x[:half] + pltpu.roll(x[half:], width - half, 1)
            half //= 2
        row = x[0:1]
        for i in range(1, 8):
            row = row + pltpu.roll(x[i : i + 1], width - i, 1)
        drel_ref[0, h : h + 1, :] = row


def attention_specs(rows, width, pairs):
    return [
        pl.BlockSpec((1, 2, width), lambda j, own: (j, 0, 0)),
        pl.BlockSpec((rows, 128), lambda j, own: (0, j)),
        pl.BlockSpec((rows, 128), lambda j, own: (0, pairs + j)),
        pl.BlockSpec((rows, 128), lambda j, own: (0, 2 * pairs + j)),
    ]


def attend(own, table, qkv, n_prompt, n_cont, group, head_size):
    pairs, _, width = table.shape
    mine = n_prompt + n_cont
    work = pairs * 2 * (n_prompt * n_prompt * group + n_cont * (n_prompt * group + n_cont))
    return pl.pallas_call(
        functools.partial(attend_kernel, n_prompt, n_cont, group, head_size),
        out_shape=(
            jax.ShapeDtypeStruct((mine, pairs * 128), bf16),
            jax.ShapeDtypeStruct((pairs, 2, mine), f32),
        ),
        grid_spec=pltpu.PrefetchScalarGridSpec(
            num_scalar_prefetch=1,
            grid=(pairs,),
            in_specs=attention_specs(qkv.shape[0], width, pairs),
            out_specs=(
                pl.BlockSpec((mine, 128), lambda j, own: (0, j)),
                pl.BlockSpec((1, 2, mine), lambda j, own: (j, 0, 0)),
            ),
            scratch_shapes=[pltpu.VMEM((2, KB, width), f32)],
        ),
        compiler_params=pltpu.CompilerParams(vmem_limit_bytes=VMEM_LIMIT),
        cost_estimate=pl.CostEstimate(flops=16 * work * head_size, bytes_accessed=16 * mine * pairs * 128, transcendentals=work),
        name="attend",
    )(own, table, qkv, qkv, qkv)


def attend_grad(own, table, qkv, heads_out, dheads, lse, n_prompt, n_cont, group, head_size):
    pairs, _, width = table.shape
    rows, mine = qkv.shape[0], n_prompt + n_cont
    work = pairs * 2 * (n_prompt * n_prompt * group + n_cont * (n_prompt * group + n_cont))
    return pl.pallas_call(
        functools.partial(attend_grad_kernel, n_prompt, n_cont, group, head_size),
        out_shape=(
            jax.ShapeDtypeStruct((3, rows, pairs * 128), bf16),
            jax.ShapeDtypeStruct((pairs, 2, width), f32),
        ),
        grid_spec=pltpu.PrefetchScalarGridSpec(
            num_scalar_prefetch=1,
            grid=(pairs,),
            in_specs=attention_specs(rows, width, pairs)
            + [
                pl.BlockSpec((mine, 128), lambda j, own: (0, j)),
                pl.BlockSpec((mine, 128), lambda j, own: (0, j)),
                pl.BlockSpec((1, 2, mine), lambda j, own: (j, 0, 0)),
            ],
            out_specs=(
                pl.BlockSpec((3, rows, 128), lambda j, own: (0, 0, j)),
                pl.BlockSpec((1, 2, width), lambda j, own: (j, 0, 0)),
            ),
            scratch_shapes=[
                pltpu.VMEM((2, KB, width), f32),
                pltpu.VMEM((2, KB, width), f32),
                pltpu.VMEM((rows, 128), f32),
                pltpu.VMEM((rows, 128), f32),
            ],
        ),
        compiler_params=pltpu.CompilerParams(vmem_limit_bytes=VMEM_LIMIT),
        cost_estimate=pl.CostEstimate(flops=40 * work * head_size, bytes_accessed=40 * mine * pairs * 128, transcendentals=work),
        name="attend_grad",
    )(own, table, qkv, qkv, qkv, heads_out, dheads, lse)


def unit_list(n_prompt, n_cont, cap_prompt, cap_cont, padded):
    if cap_prompt % 16 == 0 and cap_cont % 16 == 0:
        return ((0, n_prompt, 0, cap_prompt), (n_prompt, n_cont, cap_prompt, cap_cont))
    return ((0, n_prompt + n_cont, 0, padded),)


def slots_of(units, routes_ref, experts, padded, caps):
    found = []
    for (first, rows, slot), cap in zip(units, caps):
        numbers = lax.broadcasted_iota(jnp.int32, (experts, rows), 0)
        routes = [routes_ref[c : c + 1, first : first + rows] for c in range(2)]
        hits = [numbers == r for r in routes]
        both = jnp.where(hits[0] | hits[1], 1.0, 0.0).astype(bf16)
        before = lax.broadcasted_iota(jnp.int32, (rows, rows), 0) < lax.broadcasted_iota(jnp.int32, (rows, rows), 1)
        earlier = nn(both, jnp.where(before, 1.0, 0.0).astype(bf16))
        for c in range(2):
            count = jnp.sum(jnp.where(hits[c], earlier, 0.0), axis=0, keepdims=True).astype(jnp.int32)
            found.append(jnp.where(count < cap, routes[c] * padded + slot + count, -1))
    return found


def chosen_rows(target_ref, unit, experts, padded):
    first, rows, slot, slots = unit
    parts = []
    for e in range(experts):
        numbers = lax.broadcasted_iota(jnp.int32, (slots, rows), 0) + (e * padded + slot)
        hit = [numbers == target_ref[c : c + 1, first : first + rows] for c in range(2)]
        parts.append(jnp.where(hit[0] | hit[1], 1.0, 0.0).astype(bf16))
    return jnp.concatenate(parts, axis=0)


def target_columns(target_ref, unit):
    first, rows = unit[:2]
    turned = target_ref[:, first : first + rows].astype(f32).T.astype(jnp.int32)
    return [turned[:, c : c + 1] for c in range(2)]


def cots_kernel(units, caps, experts, padded, routes_ref, cot_refs, target_ref, out_ref):
    first_slot = 0
    row_units = []
    first = 0
    for rows, cap in caps:
        row_units.append((first, rows, first_slot))
        first, first_slot = first + rows, first_slot + cap
    found = slots_of(row_units, routes_ref, experts, padded, [cap for _, cap in caps])
    target_ref[...] = jnp.full(target_ref.shape, -1, jnp.int32)
    for u, (first, rows, _) in enumerate(row_units):
        for c in range(2):
            target_ref[c : c + 1, first : first + rows] = found[2 * u + c]
    for unit in units:
        first, rows, slot, slots = unit
        cot = jnp.concatenate([ref[...] for ref in cot_refs], axis=0) if len(units) == 1 else cot_refs[1 if first else 0][...]
        got = nn(chosen_rows(target_ref, unit, experts, padded), cot).astype(bf16)
        for e in range(experts):
            out_ref[e, slot : slot + slots, :] = got[e * slots : (e + 1) * slots]


def remote(src, dst, device, send_sem, recv_sem):
    return pltpu.make_async_remote_copy(
        src_ref=src, dst_ref=dst, send_sem=send_sem, recv_sem=recv_sem, device_id=device, device_id_type=pl.DeviceIdType.MESH
    )


def greet(devices):
    barrier = pltpu.get_barrier_semaphore()
    for device in devices:
        pl.semaphore_signal(barrier, inc=1, device_id=device, device_id_type=pl.DeviceIdType.MESH)
    pl.semaphore_wait(barrier, len(devices))


def look_up(table, i):
    found = jnp.int32(table[0])
    for j in range(1, len(table)):
        found = jnp.where(i == j, jnp.int32(table[j]), found)
    return found


def ring_places(cycle):
    count = len(cycle)
    inverse = [0] * count
    for p, c in enumerate(cycle):
        inverse[c] = p
    team = lax.axis_index("team")
    place = look_up(inverse, lax.axis_index("depth") * 2 + team // 2)

    def chip(distance):
        return look_up(cycle, lax.rem(place + (distance + count), count))

    def device(chip, core):
        return {"depth": chip // 2, "team": lax.rem(chip, 2) * 2 + core}

    return chip, device, lax.rem(team, 2)


def ring_pieces(cut, qkv, wout, extra):
    return ((qkv, slice(0, cut), 0), (qkv, slice(cut, qkv.shape[-1]), 1), (wout, slice(0, wout.shape[-1]), 1), (extra, slice(0, extra.shape[-1]), 1))


def ring_gather(cycle, cut, hops_from, hops_to, shards, outs, sems, between=()):
    ring_send, ring_recv, core_send, core_recv = sems
    count = len(cycle)
    chip, at, core = ring_places(cycle)
    right, left, partner = at(chip(1), core), at(chip(-1), core), {"team": lax.axis_index("team") + 1 - 2 * core}
    pieces = ring_pieces(cut, *outs)
    long, short = count // 2, count - 1 - count // 2
    streams = ((0, right, -1, long), (1, left, 1, long), (0, left, 1, short), (1, right, -1, short))
    started, arrivals = [], []

    def start(copy):
        copy.start()
        started.append(copy)

    def slot(p, c, k):
        return pieces[p][0].at[c, k, :, pieces[p][1]]

    def source(p, c):
        return slot(p, c, core) if shards is None else ring_pieces(cut, *shards)[p][0].at[:, pieces[p][1]]

    def hop_copies(k, c, hop, first=False):
        half, device = streams[k][:2]
        return [
            remote(source(p, c) if first else slot(p, c, core), slot(p, c, core), device, ring_send.at[k, hop, p], ring_recv.at[k, hop, p])
            for p in range(len(pieces))
            if pieces[p][2] == half
        ]

    def across(c, half, first=False):
        for p in range(len(pieces)):
            if pieces[p][2] == half:
                number = len(arrivals)
                start(remote(source(p, c) if first else slot(p, c, core), slot(p, c, core), partner, core_send.at[number], core_recv.at[number]))
                arrivals.append(slot(p, c, 1 - core))

    for k, (half, device, sign, hops) in enumerate(streams):
        if hops_from < hops:
            for copy in hop_copies(k, chip(sign * hops_from), hops_from, hops_from == 0):
                start(copy)
    if hops_from == 0:
        for half in range(2):
            across(chip(0), half, True)
    for action in between:
        action()
    for hop in range(hops_from, hops_to):
        for k, (half, device, sign, hops) in enumerate(streams):
            if hop < hops:
                other = chip(sign * (1 + hop))
                for copy in hop_copies(k, other, hop):
                    copy.wait_recv()
                if hop + 1 < min(hops, hops_to):
                    for copy in hop_copies(k, other, hop + 1):
                        start(copy)
                across(other, half)
    waits = [remote(v, v, partner, core_send.at[n], core_recv.at[n]).wait_recv for n, v in enumerate(arrivals)]
    return waits + [copy.wait_send for copy in started]


def ring_neighbours(cycle):
    chip, at, core = ring_places(cycle)
    return [at(chip(1), core), at(chip(-1), core), {"team": lax.axis_index("team") + 1 - 2 * core}]


def front_kernel(cycle, cut, hops, qkv_ref, wout_ref, extra_ref, win_ref, qkv_out, wout_out, extra_out, win_out,
                 ring_send, ring_recv, core_send, core_recv, team_send, team_recv, local_sem):
    chip, _, core = ring_places(cycle)
    team = lax.axis_index("team")
    mates = [team + d - 4 * ((team + d) // 4) for d in range(1, 4)]
    greet(ring_neighbours(cycle) + [{"team": t} for t in mates])
    waits = []

    def swap():
        for d, t in enumerate(mates):
            copy = remote(win_ref.at[t], win_out.at[team], {"team": t}, team_send.at[d], team_recv.at[d])
            copy.start()
            source = team + 3 - d - 4 * ((team + 3 - d) // 4)
            waits.append(remote(win_ref.at[t], win_out.at[source], {"team": t}, team_send.at[d], team_recv.at[d]).wait_recv)
            waits.append(copy.wait_send)
        keep = [(win_ref.at[team], win_out.at[team])]
        keep += [(src, out.at[chip(0), core]) for src, out in ((qkv_ref, qkv_out), (wout_ref, wout_out), (extra_ref, extra_out))]
        for p, (src, dst) in enumerate(keep):
            copy = pltpu.make_async_copy(src, dst, local_sem.at[p])
            copy.start()
            waits.append(copy.wait)

    outs = (qkv_out, wout_out, extra_out)
    sems = (ring_send, ring_recv, core_send, core_recv)
    waits += ring_gather(cycle, cut, 0, hops, (qkv_ref, wout_ref, extra_ref), outs, sems, (swap,))
    for wait in waits:
        wait()


def front_rest_kernel(cycle, group, fixed, cut, hops, qkv_in, wout_in, extra_in, x_ref, routes_ref, prompt_cot_ref, cont_cot_ref,
                      qkv_out, wout_out, extra_out, x_out, target_ref, cots_ref,
                      ring_send, ring_recv, core_send, core_recv, row_send, row_recv):
    own = lax.axis_index("expert")
    rows = [lax.rem(own + s, group) for s in range(1, group)]
    greet(ring_neighbours(cycle) + [{"expert": g} for g in rows])
    waits = []

    def others():
        for s, g in enumerate(rows):
            back = lax.rem(own + group - (s + 1), group)
            copy = remote(x_ref, x_out.at[s], {"expert": back}, row_send.at[s], row_recv.at[s])
            copy.start()
            waits.append(remote(x_ref, x_out.at[s], {"expert": g}, row_send.at[s], row_recv.at[s]).wait_recv)
            waits.append(copy.wait_send)
        cots_kernel(*fixed, routes_ref, (prompt_cot_ref, cont_cot_ref), target_ref, cots_ref)

    outs = (qkv_out, wout_out, extra_out)
    sems = (ring_send, ring_recv, core_send, core_recv)
    waits += ring_gather(cycle, cut, hops, len(cycle) // 2, None, outs, sems, (others,))
    for wait in waits:
        wait()


def front(w_qkv, w_out, extra, expert_in, x_prompt, routes, prompt_cot, cont_cot, fixed, cycle, group):
    count = len(cycle)
    experts, padded = fixed[2:]
    rows, columns = w_qkv.shape
    cut = (columns + w_out.shape[1] + extra.shape[1]) // 256 * 128
    hops = count // 4
    anywhere, vmem = pl.BlockSpec(memory_space=pl.ANY), pl.BlockSpec(memory_space=pltpu.VMEM)
    ring_sems = [pltpu.SemaphoreType.DMA((4, count, 4))] * 2 + [pltpu.SemaphoreType.DMA((4 * count,))] * 2
    dense_shapes = tuple(jax.ShapeDtypeStruct((count, 2) + v.shape, bf16) for v in (w_qkv, w_out, extra))
    cost = pl.CostEstimate(flops=10**10, bytes_accessed=10**8, transcendentals=0)
    *dense, w_in = pl.pallas_call(
        functools.partial(front_kernel, cycle, cut, hops),
        out_shape=dense_shapes + (jax.ShapeDtypeStruct(expert_in.shape, bf16),),
        in_specs=[anywhere] * 4,
        out_specs=(anywhere,) * 4,
        scratch_shapes=ring_sems + [pltpu.SemaphoreType.DMA((3,))] * 2 + [pltpu.SemaphoreType.DMA((4,))],
        compiler_params=pltpu.CompilerParams(collective_id=0, has_side_effects=True, vmem_limit_bytes=VMEM_LIMIT),
        cost_estimate=cost,
        name="front",
    )(w_qkv, w_out, extra, expert_in)
    results = pl.pallas_call(
        functools.partial(front_rest_kernel, cycle, group, fixed, cut, hops),
        out_shape=dense_shapes
        + (
            jax.ShapeDtypeStruct((group - 1,) + x_prompt.shape, bf16),
            jax.ShapeDtypeStruct(routes.shape, jnp.int32),
            jax.ShapeDtypeStruct((experts, padded, prompt_cot.shape[1]), bf16),
        ),
        in_specs=[anywhere] * 4 + [vmem] * 3,
        out_specs=(anywhere,) * 4 + (vmem,) * 2,
        scratch_shapes=ring_sems + [pltpu.SemaphoreType.DMA((group,))] * 2,
        input_output_aliases={0: 0, 1: 1, 2: 2},
        compiler_params=pltpu.CompilerParams(collective_id=4, has_side_effects=True, vmem_limit_bytes=VMEM_LIMIT),
        cost_estimate=cost,
        name="front_rest",
    )(*dense, x_prompt, routes, prompt_cot, cont_cot)
    return [v.reshape(count * 2 * rows, v.shape[3]) for v in results[:3]] + [w_in] + list(results[3:])


def team_ring(group):
    team, own = lax.axis_index("team"), lax.axis_index("expert")

    def peer(i):
        g, t = lax.rem(own + i // 4, group), lax.rem(team + lax.rem(i, 4), 4)
        return g * 4 + t, {"team": t, "expert": g}

    def back_from(i):
        return lax.rem(own + (group - i // 4), group) * 4 + lax.rem(team + (4 - lax.rem(i, 4)), 4)

    return own * 4 + team, peer, back_from


def expert_up_kernel(units, group, experts, padded, target_ref, gate_ref, routes_ref, z_ref, cots_ref, w_in_ref,
                     active_hbm, slope_hbm, grad_hbm, dproduced_ref, arrived_t_ref,
                     stage_ref, gate_stage, arrived_ref, gate_in, held_ref, chunk_ref, dproduced_t_ref, tile_ref, row_send, row_recv, gate_send, gate_recv, held_sem, chunk_sem, tile_sem):
    me, peer, back_from = team_ring(group)
    sources = 4 * group
    hidden = w_in_ref.shape[1]
    step = next(n for n in (512, 256, 128) if hidden % n == 0)
    greet([peer(jnp.int32(i))[1] for i in range(1, sources)])
    for unit in units:
        first, rows, slot, slots = unit
        chosen = chosen_rows(target_ref, unit, experts, padded)
        got = nn(chosen, z_ref[first : first + rows, :]).astype(bf16)
        features = []
        for c in range(2):
            left = gate_ref[c : c + 1, first : first + rows]
            for _ in range(3):
                low = left.astype(bf16).astype(f32)
                features.append(low)
                left = left - low
        features.append(routes_ref[0:1, first : first + rows].astype(f32))
        features.append(jnp.zeros_like(features[0]))
        picked = nt(jnp.concatenate(features, axis=0).astype(bf16), chosen)
        gates = [picked[3 * c : 3 * c + 1] + picked[3 * c + 1 : 3 * c + 2] + picked[3 * c + 2 : 3 * c + 3] for c in range(2)]
        for e in range(experts):
            part = slice(e * slots, (e + 1) * slots)
            stage_ref[e, slot : slot + slots, :] = got[part]
            gate = jnp.where(picked[6:7, part] == float(e), gates[0][:, part], gates[1][:, part])
            gate_stage[e, :, slot : slot + slots] = jnp.broadcast_to(gate, (8, slots))

    def sends(i, to):
        number, device = peer(i)
        return (
            remote(gate_stage.at[number], gate_in.at[to], device, gate_send.at[i], gate_recv.at[i]),
            remote(stage_ref.at[number], arrived_ref.at[to], device, row_send.at[i], row_recv.at[i]),
        )

    for i in range(1, sources):
        for copy in sends(jnp.int32(i), me):
            copy.start()
    arrived_ref[me] = stage_ref[me]
    gate_in[me] = gate_stage[me]

    def keep(number, slot):
        return pltpu.make_async_copy(chunk_ref.at[slot], slope_hbm.at[number], chunk_sem.at[slot])

    def out(number):
        return pltpu.make_async_copy(held_ref.at[number], active_hbm.at[number], held_sem.at[number])

    def source(i, carry):
        number, slot = back_from(i), lax.rem(i, 2)

        @pl.when(i > 0)
        def _():
            for copy in sends(i, number):
                copy.wait_recv()

        @pl.when(i >= 2)
        def _():
            keep(back_from(i - 2), slot).wait()

        dproduced_ref[number] = (cots_ref[number].astype(f32) * gate_in[number].T[:, 0:1]).astype(bf16)
        arrived = arrived_ref[number]
        for first in range(0, hidden, step):
            at = slice(first, first + step)
            active, slope = gelu_parts(nn(arrived, w_in_ref[:, at]))
            chunk_ref[slot, :, at] = slope.astype(bf16)
            held_ref[number, :, at] = active.astype(bf16)
        keep(number, slot).start()
        out(number).start()
        return carry

    lax.fori_loop(0, sources, source, 0)
    width = dproduced_ref.shape[2]
    dproduced_t_ref[...] = dproduced_ref[...].reshape(-1, width).T
    arrived_t_ref[...] = arrived_ref[...].reshape(-1, width).T

    def put(f):
        at = pl.ds(pl.multiple_of(f * step, step), step)
        return pltpu.make_async_copy(tile_ref.at[lax.rem(f, 2)], grad_hbm.at[at, :], tile_sem.at[lax.rem(f, 2)])

    def product(f, carry):
        @pl.when(f >= 2)
        def _():
            put(f - 2).wait()

        active = held_ref[:, :, pl.ds(pl.multiple_of(f * step, step), step)].reshape(-1, step)
        tile_ref[lax.rem(f, 2)] = nn(dproduced_t_ref[...], active).astype(bf16).T
        put(f).start()
        return carry

    steps = hidden // step
    lax.fori_loop(0, steps, product, 0)
    for f in range(max(0, steps - 2), steps):
        put(jnp.int32(f)).wait()
    for i in range(sources - 2, sources):
        keep(back_from(jnp.int32(i)), jnp.int32(i % 2)).wait()
    for i in range(sources):
        out(back_from(jnp.int32(i))).wait()
    for i in range(1, sources):
        for copy in sends(jnp.int32(i), me):
            copy.wait_send()


def expert_up(target, gates, routes, z, cots, w_in, units, group, experts, padded):
    sources = 4 * group
    width, hidden = w_in.shape
    step = next(n for n in (512, 256, 128) if hidden % n == 0)
    slots = sources * padded
    anywhere, vmem = pl.BlockSpec(memory_space=pl.ANY), pl.BlockSpec(memory_space=pltpu.VMEM)
    return pl.pallas_call(
        functools.partial(expert_up_kernel, units, group, experts, padded),
        out_shape=(
            jax.ShapeDtypeStruct((sources, padded, hidden), bf16),
            jax.ShapeDtypeStruct((sources, padded, hidden), bf16),
            jax.ShapeDtypeStruct((hidden, width), bf16),
            jax.ShapeDtypeStruct((sources, padded, width), bf16),
            jax.ShapeDtypeStruct((width, slots), bf16),
        ),
        in_specs=[vmem] * 6,
        out_specs=(anywhere,) * 3 + (vmem,) * 2,
        scratch_shapes=[
            pltpu.VMEM((experts, padded, width), bf16),
            pltpu.VMEM((experts, 8, padded), f32),
            pltpu.VMEM((sources, padded, width), bf16),
            pltpu.VMEM((sources, 8, padded), f32),
            pltpu.VMEM((sources, padded, hidden), bf16),
            pltpu.VMEM((2, padded, hidden), bf16),
            pltpu.VMEM((width, slots), bf16),
            pltpu.VMEM((2, step, width), bf16),
        ]
        + [pltpu.SemaphoreType.DMA((sources,))] * 5
        + [pltpu.SemaphoreType.DMA((2,))] * 2,
        compiler_params=pltpu.CompilerParams(collective_id=1, has_side_effects=True, vmem_limit_bytes=VMEM_LIMIT),
        cost_estimate=pl.CostEstimate(flops=6 * slots * width * hidden, bytes_accessed=10**8, transcendentals=0),
        name="expert_up",
    )(target, gates, routes, z, cots, w_in)


def expert_back_kernel(units, group, experts, padded, target_ref, dproduced_hbm, slope_hbm, active_hbm, arrived_t_ref, w_in_ref, w_down_ref,
                       grad_hbm, dz_ref, inner_ref, dbefore_ref, stage_ref, back_ref, inner_stage, inner_back, tile_ref,
                       active_ref, copy_sem, active_sem, tile_sem, row_send, row_recv, inner_send, inner_recv):
    me, peer, back_from = team_ring(group)
    sources = 4 * group
    hidden = w_in_ref.shape[1]
    tile = next(t for t in (768, 512, 256) if hidden % t == 0)

    def load(i):
        number = peer(i)[0]
        return (
            pltpu.make_async_copy(slope_hbm.at[number], dbefore_ref.at[number], copy_sem.at[0, i]),
            pltpu.make_async_copy(dproduced_hbm.at[number], stage_ref.at[number], copy_sem.at[1, i]),
        )

    def sends(i, to):
        number, device = peer(i)
        return (
            remote(inner_stage.at[number], inner_back.at[to], device, inner_send.at[i], inner_recv.at[i]),
            remote(stage_ref.at[number], back_ref.at[to], device, row_send.at[i], row_recv.at[i]),
        )

    def fetch(turn):
        slot = lax.rem(turn, 2)
        return pltpu.make_async_copy(active_hbm.at[peer(lax.rem(turn + 1, sources))[0]], active_ref.at[slot], active_sem.at[slot])

    for i in list(range(1, sources)) + [0]:
        for copy in load(jnp.int32(i)):
            copy.start()
        if i in (1, 2):
            fetch(jnp.int32(i - 1)).start()
    greet([peer(jnp.int32(i))[1] for i in range(1, sources)])

    def source(step, carry):
        i = lax.rem(step + 1, sources)
        number, slot = peer(i)[0], lax.rem(step, 2)
        for copy in load(i):
            copy.wait()
        fetch(step).wait()
        dproduced = stage_ref[number]
        inner = darrived = None
        for first in range(0, hidden, tile):
            at = slice(first, first + tile)
            dactive = nt(dproduced, w_down_ref[at, :])
            product = active_ref[slot, :, at].astype(f32) * dactive
            for lane in range(0, tile, 128):
                part = product[:, lane : lane + 128]
                inner = part if inner is None else inner + part
            dbefore = (dactive * dbefore_ref[number, :, at].astype(f32)).astype(bf16)
            dbefore_ref[number, :, at] = dbefore
            part = nt(dbefore, w_in_ref[:, at])
            darrived = part if darrived is None else darrived + part

        @pl.when(step + 2 < sources)
        def _():
            fetch(step + 2).start()

        inner_stage[number] = jnp.broadcast_to(jnp.sum(inner, axis=1, keepdims=True), (padded, 128)).T[:8]
        stage_ref[number] = darrived.astype(bf16)

        @pl.when(step + 1 < sources)
        def _():
            for copy in sends(i, me):
                copy.start()

        return carry

    lax.fori_loop(0, sources, source, 0)
    back_ref[me] = stage_ref[me]
    inner_back[me] = inner_stage[me]
    wide = next(n for n in (512, 256, 128) if hidden % n == 0)
    steps = hidden // wide

    def put(f):
        at = pl.ds(pl.multiple_of(f * wide, wide), wide)
        return pltpu.make_async_copy(tile_ref.at[lax.rem(f, 2)], grad_hbm.at[:, at], tile_sem.at[lax.rem(f, 2)])

    def product(f, carry):
        @pl.when(f >= 2)
        def _():
            put(f - 2).wait()

        dbefore = dbefore_ref[:, :, pl.ds(pl.multiple_of(f * wide, wide), wide)].reshape(-1, wide)
        tile_ref[lax.rem(f, 2)] = nn(arrived_t_ref[...], dbefore).astype(bf16)
        put(f).start()
        return carry

    lax.fori_loop(0, steps, product, 0)
    for f in range(max(0, steps - 2), steps):
        put(jnp.int32(f)).wait()
    for i in range(1, sources):
        sends(jnp.int32(i), back_from(jnp.int32(i)))[0].wait_recv()

    def hits(unit, columns, e):
        first, rows, slot, slots = unit
        numbers = lax.broadcasted_iota(jnp.int32, (rows, slots), 1) + (e * padded + slot)
        return [numbers == column for column in columns]

    for unit in units:
        first, rows, slot, slots = unit
        columns = target_columns(target_ref, unit)
        sums = [0.0, 0.0]
        for e in range(experts):
            inner = inner_back[e, 0:1, slot : slot + slots]
            for c, hit in enumerate(hits(unit, columns, e)):
                sums[c] = sums[c] + jnp.sum(jnp.where(hit, inner, 0.0), axis=1, keepdims=True)
        lanes = lax.broadcasted_iota(jnp.int32, (rows, 128), 1)
        both = jnp.where(lanes == 0, sums[0], jnp.where(lanes == 1, sums[1], 0.0))
        inner_ref[:, first : first + rows] = both.T[:8]
    for i in range(1, sources):
        sends(jnp.int32(i), back_from(jnp.int32(i)))[1].wait_recv()
    for unit in units:
        first, rows, slot, slots = unit
        columns = target_columns(target_ref, unit)
        total = None
        for e in range(experts):
            hit = hits(unit, columns, e)
            part = nn(jnp.where(hit[0] | hit[1], 1.0, 0.0).astype(bf16), back_ref[e, slot : slot + slots, :])
            total = part if total is None else total + part
        dz_ref[first : first + rows, :] = total
    for i in range(1, sources):
        for copy in sends(jnp.int32(i), me):
            copy.wait_send()


def expert_back(target, dproduced, slope, active, arrived_t, w_in, w_down, units, group, experts, padded):
    sources, mine = 4 * group, target.shape[1]
    width, hidden = w_in.shape
    anywhere, vmem = pl.BlockSpec(memory_space=pl.ANY), pl.BlockSpec(memory_space=pltpu.VMEM)
    return pl.pallas_call(
        functools.partial(expert_back_kernel, units, group, experts, padded),
        out_shape=(
            jax.ShapeDtypeStruct((width, hidden), bf16),
            jax.ShapeDtypeStruct((mine, width), f32),
            jax.ShapeDtypeStruct((8, mine), f32),
        ),
        in_specs=[vmem, anywhere, anywhere, anywhere] + [vmem] * 3,
        out_specs=(anywhere, vmem, vmem),
        scratch_shapes=[
            pltpu.VMEM((sources, padded, hidden), bf16),
            pltpu.VMEM((sources, padded, width), bf16),
            pltpu.VMEM((experts, padded, width), bf16),
            pltpu.VMEM((sources, 8, padded), f32),
            pltpu.VMEM((experts, 8, padded), f32),
            pltpu.VMEM((2, width, 512 if hidden % 512 == 0 else 256 if hidden % 256 == 0 else 128), bf16),
            pltpu.VMEM((2, padded, hidden), bf16),
            pltpu.SemaphoreType.DMA((2, sources)),
            pltpu.SemaphoreType.DMA((2,)),
            pltpu.SemaphoreType.DMA((2,)),
        ]
        + [pltpu.SemaphoreType.DMA((sources,))] * 4,
        compiler_params=pltpu.CompilerParams(collective_id=2, has_side_effects=True, vmem_limit_bytes=VMEM_LIMIT),
        cost_estimate=pl.CostEstimate(flops=6 * sources * padded * width * hidden, bytes_accessed=10**8, transcendentals=0),
        name="expert_back",
    )(target, dproduced, slope, active, arrived_t, w_in, w_down)


def mix_rows(unit, experts, padded, target_ref, gate_ref, middle_ref, back_ref, out_ref):
    first, rows, slot, slots = unit
    columns = target_columns(target_ref, unit)
    turned = gate_ref[:, first : first + rows].T
    total = middle_ref[first : first + rows, :]
    for e in range(experts):
        numbers = lax.broadcasted_iota(jnp.int32, (rows, slots), 1) + (e * padded + slot)
        weight = sum(jnp.where(numbers == columns[c], turned[:, c : c + 1], 0.0) for c in range(2))
        total = total + nn(weight.astype(bf16), back_ref[e, slot : slot + slots, :])
    out_ref[first : first + rows, :] = total.astype(bf16)


def finish_kernel(cycle, group, n_prompt, units, experts, padded, *refs):
    parts, refs = refs[:3], refs[3:]
    win_ref, gain_ref, target_ref, gate_ref = refs[:4]
    brought, refs = refs[4:10], refs[10:]
    outs, refs = refs[:3], refs[3:]
    win_out, dx_ref, mixed_ref = refs[:3]
    got, send_refs, recv_refs, rows_refs = refs[3:6], refs[6:11], refs[11:16], refs[16:19]
    away_ref, home_ref = refs[19:21]
    held, refs = refs[21:27], refs[27:]
    core_send, core_recv, ring_send, ring_recv, row_send, row_recv, team_send, team_recv, away_send, away_recv, local_sem, bring_sem = refs
    dqkv_ref, w_ref, x_ref, dmiddle_ref, middle_ref, back_ref = held
    sources = list(brought)
    sources[2] = sources[2].at[: x_ref.shape[0], :]
    bring = [pltpu.make_async_copy(src, dst, bring_sem.at[k]) for k, (src, dst) in enumerate(zip(sources, held))]
    for copy in bring:
        copy.start()
    count = len(cycle)
    chip, at, core = ring_places(cycle)
    own, team = lax.axis_index("expert"), lax.axis_index("team")
    right, left, partner = at(chip(1), core), at(chip(-1), core), {"team": team + 1 - 2 * core}
    peers = [{"expert": lax.rem(own + s, group)} for s in range(1, group)]
    mates = [team + d - 4 * ((team + d) // 4) for d in range(1, 4)]
    greet([right, left, partner] + peers + [{"team": t} for t in mates])
    started, ends = [], []

    def start(copy):
        copy.start()
        started.append(copy)

    order = []
    for hop in range(count - 1):
        for distance in (-1 - hop, 1 + hop):
            if (distance + count) % count not in order:
                order.append((distance + count) % count)
    order.append(0)

    def core_copies(number, c):
        return [
            remote(part.at[:, c, 1 - core], got[k].at[c], partner, core_send.at[k, number], core_recv.at[k, number])
            for k, part in enumerate(parts)
        ]

    for number, distance in enumerate(order):
        for copy in core_copies(number, chip(distance)):
            start(copy)
    waited = []

    def ready(distance):
        number = order.index((distance + count) % count)
        if number not in waited:
            waited.append(number)
            for copy in core_copies(number, chip(distance)):
                copy.wait_recv()
        return chip(distance)

    streams = ((0, 0, 1, right, -1), (0, 2, 1, left, 1), (0, 1, 1, right, -1), (1, 0, 1, left, 1), (2, 0, 1, left, 1))

    def hop_on(hop):
        for way, (k, lo, blocks, device, sign) in enumerate(streams):
            c = ready(sign * (1 + hop))
            for i in range(blocks):
                total = parts[k][lo + i, c, core].astype(f32) + got[k][c, lo + i].astype(f32)
                if hop:
                    if i == 0:
                        slot = recv_refs[way].at[hop - 1]
                        remote(slot, slot, device, ring_send.at[way, hop - 1], ring_recv.at[way, hop - 1]).wait_recv()
                    total = total + recv_refs[way][hop - 1, i].astype(f32)
                if hop < count - 1:
                    send_refs[way][hop, i] = total.astype(bf16)
                else:
                    rows_refs[k][own, lo + i] = total.astype(bf16)
            if hop < count - 1:
                start(remote(send_refs[way].at[hop], recv_refs[way].at[hop], device, ring_send.at[way, hop], ring_recv.at[way, hop]))

    def swap():
        for d, t in enumerate(mates):
            start(remote(win_ref.at[t], win_out.at[team], {"team": t}, team_send.at[d], team_recv.at[d]))
            source = team + 3 - d - 4 * ((team + 3 - d) // 4)
            ends.append(remote(win_ref.at[t], win_out.at[source], {"team": t}, team_send.at[d], team_recv.at[d]))
        keep = pltpu.make_async_copy(win_ref.at[team], win_out.at[team], local_sem)
        keep.start()
        keeps.append(keep)

    keeps, here = [], []

    def have(*numbers):
        for k in numbers:
            if k not in here:
                here.append(k)
                bring[k].wait()

    mine, width = dx_ref.shape
    chunk = 256 if n_prompt % 256 == 0 and mine % 256 == 0 else 128

    def front_rows(first):
        have(0, 1)
        return sum(
            nt(dqkv_ref[c, first : first + chunk, :], w_ref[:, c * width : (c + 1) * width]) for c in range(3)
        )

    def away_chunk(first):
        s, row = first // n_prompt, first % n_prompt
        away_ref[s, row : row + chunk, :] = front_rows(mine + first).astype(bf16)
        if row + chunk == n_prompt:
            start(remote(away_ref.at[s], home_ref.at[s], peers[s], away_send.at[s], away_recv.at[s]))

    def own_chunk(first):
        dx_ref[first : first + chunk, :] = front_rows(first)

    def last_chunk(first):
        have(2, 3)
        at = slice(first, first + chunk)
        x = x_ref[at, :].astype(f32)
        inverse = lax.rsqrt(jnp.mean(x * x, axis=-1, keepdims=True) + epsilon)
        unit = x * inverse
        dnormed = dx_ref[at, :]
        if first < n_prompt:
            for s in range(group - 1):
                dnormed = dnormed + home_ref[s, at, :].astype(f32)
        dunit = dnormed * gain_ref[0:1, :]
        dx_ref[at, :] = dmiddle_ref[at, :] + inverse * (dunit - unit * jnp.mean(dunit * unit, axis=-1, keepdims=True))

    fillers = [functools.partial(away_chunk, first) for first in range(0, (group - 1) * n_prompt, chunk)]
    fillers += [functools.partial(own_chunk, first) for first in range(0, mine, chunk)]

    def mix(unit):
        have(4, 5)
        mix_rows(unit, experts, padded, target_ref, gate_ref, middle_ref, back_ref, mixed_ref)

    fillers += [functools.partial(mix, unit) for unit in units]
    fillers += [functools.partial(last_chunk, first) for first in range(n_prompt, mine, chunk)]
    for hop in range(count - 1):
        hop_on(hop)
        if hop == 0:
            swap()
        for filler in fillers[hop * len(fillers) // (count - 1) : (hop + 1) * len(fillers) // (count - 1)]:
            filler()
    hop_on(count - 1)
    for s, peer in enumerate(peers):
        for k, rows in enumerate(rows_refs):
            start(remote(rows.at[own], rows.at[own], peer, row_send.at[k, s], row_recv.at[k, s]))
    for s in range(1, group):
        remote(away_ref.at[s - 1], home_ref.at[s - 1], peers[s - 1], away_send.at[s - 1], away_recv.at[s - 1]).wait_recv()
    for first in range(0, n_prompt, chunk):
        last_chunk(first)
    for s in range(1, group):
        other = lax.rem(own + group - s, group)
        for k, rows in enumerate(rows_refs):
            remote(rows.at[other], rows.at[other], peers[s - 1], row_send.at[k, s - 1], row_recv.at[k, s - 1]).wait_recv()
    for out, rows in zip(outs, rows_refs):
        for i in range(rows.shape[1]):
            total = rows[0, i].astype(f32)
            for j in range(1, group):
                total = total + rows[j, i].astype(f32)
            out[:, i * rows.shape[3] : (i + 1) * rows.shape[3]] = total
    for copy in ends:
        copy.wait_recv()
    for copy in started:
        copy.wait_send()
    for copy in keeps:
        copy.wait()


def finish(parts, grad_in, gain, target, gates, dqkv, w_qkv, x, dmiddle, middle, back, n_prompt, units, padded, cycle, group):
    count = len(cycle)
    depth = parts[0].shape[1]
    rows = depth // (2 * count)
    mine, width = dmiddle.shape
    experts = back.shape[0]
    shapes = [(v.shape[0], v.shape[2]) for v in parts]
    streams = [(1, shapes[0][1])] * 3 + [shapes[1], shapes[2]]
    anywhere, vmem = pl.BlockSpec(memory_space=pl.ANY), pl.BlockSpec(memory_space=pltpu.VMEM)
    ring = [pltpu.VMEM((count - 1, k, rows, n), bf16) for k, n in streams]
    return pl.pallas_call(
        functools.partial(finish_kernel, cycle, group, n_prompt, units, experts, padded),
        out_shape=tuple(jax.ShapeDtypeStruct((rows, k * n), f32) for k, n in shapes)
        + (
            jax.ShapeDtypeStruct(grad_in.shape, bf16),
            jax.ShapeDtypeStruct((mine, width), f32),
            jax.ShapeDtypeStruct((mine, width), bf16),
        ),
        in_specs=[vmem] * 3 + [anywhere] + [vmem] * 3 + [anywhere] * 6,
        out_specs=(vmem,) * 3 + (anywhere,) + (vmem,) * 2,
        scratch_shapes=[pltpu.VMEM((count, k, rows, n), bf16) for k, n in shapes]
        + ring
        + ring
        + [pltpu.VMEM((group, k, rows, n), bf16) for k, n in shapes]
        + [pltpu.VMEM((group - 1, n_prompt, width), bf16)] * 2
        + [
            pltpu.VMEM(dqkv.shape, bf16),
            pltpu.VMEM((depth, 3 * width), bf16),
            pltpu.VMEM((mine, width), bf16),
            pltpu.VMEM((mine, width), f32),
            pltpu.VMEM((mine, width), f32),
            pltpu.VMEM(back.shape, bf16),
        ]
        + [pltpu.SemaphoreType.DMA((3, count))] * 2
        + [pltpu.SemaphoreType.DMA((5, count))] * 2
        + [pltpu.SemaphoreType.DMA((3, group))] * 2
        + [pltpu.SemaphoreType.DMA((3,))] * 2
        + [pltpu.SemaphoreType.DMA((group,))] * 2
        + [pltpu.SemaphoreType.DMA, pltpu.SemaphoreType.DMA((6,))],
        compiler_params=pltpu.CompilerParams(collective_id=3, has_side_effects=True, vmem_limit_bytes=VMEM_LIMIT),
        cost_estimate=pl.CostEstimate(flops=3 * 10**10, bytes_accessed=10**8, transcendentals=0),
        name="finish",
    )(
        *[v.reshape(v.shape[0], count, 2, rows, v.shape[2]) for v in parts],
        grad_in,
        gain,
        target,
        gates,
        dqkv,
        w_qkv,
        x,
        dmiddle,
        middle,
        back,
    )


def scatter_expert(grad):
    return lax.psum_scatter(grad, "depth", scatter_dimension=0, tiled=True).reshape(4, -1, grad.shape[1])


def whole_kernel(kernel, out_shape, flops, name, *args):
    return pl.pallas_call(
        kernel,
        out_shape=out_shape,
        compiler_params=pltpu.CompilerParams(vmem_limit_bytes=VMEM_LIMIT),
        cost_estimate=pl.CostEstimate(flops=flops, bytes_accessed=sum(a.size * a.dtype.itemsize for a in args), transcendentals=0),
        name=name,
    )(*args)


def gelu_parts(x):
    a = 0.7978845608028654
    square = x * x
    t = jnp.tanh(x * (a + (a * 0.044715) * square))
    half = 0.5 + 0.5 * t
    return x * half, half + (0.5 * x) * (1.0 - t * t) * (a + (3 * a * 0.044715) * square)


def rms_inverse(x):
    return lax.rsqrt(jnp.mean(x * x, axis=-1, keepdims=True) + epsilon)


def rms_grad(x, inverse, gain, dnormed):
    unit = x * inverse
    dunit = dnormed * gain
    dx = inverse * (dunit - unit * jnp.mean(dunit * unit, axis=-1, keepdims=True))
    return dx, jnp.sum(dnormed * unit, axis=0)


def per_device(
    cycle,
    prompt_in,
    cont_in,
    prompt_cot,
    cont_cot,
    prompt_route,
    cont_route,
    rel_bucket,
    norm_attn,
    norm_ffn,
    w_qkv,
    w_out,
    rel_w,
    w_router,
    expert_in,
    expert_out,
):
    shard = w_qkv.shape[0]
    fsdp = lax.axis_size("depth") * lax.axis_size("team")
    group = lax.axis_size("expert")
    width = shard * fsdp
    head_count = rel_w.shape[1]
    head_size = width // head_count
    pairs = head_count // 2
    experts = w_router.shape[1]
    n_prompt, n_cont = prompt_in.shape[1], cont_in.shape[2]
    mine, prompt_len = n_prompt + n_cont, n_prompt * group
    cap_prompt = (10 * n_prompt + 4 * experts - 1) // (4 * experts)
    cap_cont = (10 * n_cont + 4 * experts - 1) // (4 * experts)
    padded = (cap_prompt + cap_cont + 15) // 16 * 16
    units = unit_list(n_prompt, n_cont, cap_prompt, cap_cont, padded)
    own = lax.axis_index("expert")
    own_list = jnp.reshape(own, (1,)).astype(jnp.int32)

    rel_rows = rel_w.shape[0] * head_count
    extra = [
        w_router,
        norm_attn[:, None],
        norm_ffn[:, None],
        jnp.pad(rel_w.reshape(-1), (0, shard - rel_rows))[:, None],
        jnp.zeros((shard, 128 - experts - 3), bf16),
    ]
    routes = jnp.concatenate([prompt_route[0], cont_route[0, 0]]).T
    routes = jnp.pad(routes, ((0, 6), (0, 0)), constant_values=-1)
    fixed = (units, ((n_prompt, cap_prompt), (n_cont, cap_cont)), experts, padded)
    qkv_full, out_full, misc, w_in, x_other, target, cot_slots = front(
        w_qkv, w_out, jnp.concatenate(extra, axis=1), expert_in, prompt_in[0], routes, prompt_cot[0], cont_cot[0, 0], fixed, cycle, group
    )
    w_in = lax.all_gather(w_in.reshape(-1, w_in.shape[2]), "depth", axis=0, tiled=True)
    expert_out, qkv_full = lax.optimization_barrier((expert_out, qkv_full))
    w_down = lax.all_to_all(expert_out, "team", split_axis=0, concat_axis=0, tiled=True)
    cots = lax.all_to_all(cot_slots, ("expert", "team"), split_axis=0, concat_axis=0, tiled=True)
    cot = jnp.concatenate([prompt_cot[0], cont_cot[0, 0]]).astype(f32)
    router_full = misc[:, :experts]
    gain_attn = misc[:, experts].astype(f32)
    gain_ffn = misc[:, experts + 1].astype(f32)
    rel_full = misc[:, experts + 2].reshape(fsdp, shard)[:, :rel_rows].reshape(-1, head_count)
    buckets = rel_full.shape[0]

    x_low = jnp.concatenate([prompt_in[0], cont_in[0, 0], x_other.reshape(-1, width)])
    x_all = x_low.astype(f32)
    x = x_all[:mine]
    bucket_hot = (rel_bucket[None, :] == jnp.arange(buckets, dtype=jnp.int32)[:, None]).astype(f32)
    dist_table = jnp.einsum("bt,bh->ht", bucket_hot, rel_full.astype(f32), precision=lax.Precision.HIGHEST)
    table = jnp.concatenate([jnp.full((head_count, prompt_len), blocked, f32), dist_table], axis=1)
    table = table.reshape(pairs, 2, -1)
    inverse_x = rms_inverse(x_all)
    normed = (x_all * inverse_x * gain_attn).astype(bf16)
    qkv = jnp.dot(normed, qkv_full, preferred_element_type=f32).astype(bf16)
    heads_out, lse = attend(own_list, table, qkv, n_prompt, n_cont, group, head_size)
    w_down, cots, heads_out = lax.optimization_barrier((w_down, cots, heads_out))
    w_down = lax.all_gather(w_down.reshape(-1, w_down.shape[2]), "depth", axis=0, tiled=True)

    middle = x + jnp.dot(heads_out, out_full, preferred_element_type=f32)
    inverse_m = rms_inverse(middle)
    normed_ffn = (middle * inverse_m * gain_ffn).astype(bf16)
    logits = lax.dot_general(router_full, normed_ffn, (((0,), (1,)), ((), ())), preferred_element_type=f32)
    hot = [(jnp.arange(experts, dtype=jnp.int32)[:, None] == routes[c : c + 1]).astype(f32) for c in range(2)]
    picked = jnp.stack([jnp.sum(logits * h, axis=0) for h in hot])
    gates = jax.nn.softmax(picked, axis=0)
    gate_rows = jnp.pad(gates, ((0, 6), (0, 0)))

    active, slope, grad_down, dproduced, arrived_t = expert_up(
        target, gate_rows, routes, normed_ffn, cots, w_in, units, group, experts, padded
    )
    sum_down = scatter_expert(grad_down)
    grad_in, dnormed, inner = expert_back(target, dproduced, slope, active, arrived_t, w_in, w_down, units, group, experts, padded)
    sum_in = scatter_expert(grad_in)
    active, inner = lax.optimization_barrier((active, inner))
    dpicked = inner[:2] - gates * jnp.sum(inner[:2], axis=0, keepdims=True)
    dlogits = hot[0] * dpicked[0] + hot[1] * dpicked[1]
    terms, left = [], dlogits
    for _ in range(3):
        terms.append(left.astype(bf16))
        left = left - terms[-1].astype(f32)
    terms = jnp.concatenate(terms)
    dnormed = dnormed + lax.dot_general(
        terms, jnp.concatenate([router_full] * 3, axis=1), (((0,), (1,)), ((), ())), preferred_element_type=f32
    )
    grad_router = lax.dot_general(normed_ffn, terms, (((0,), (1,)), ((), ())), preferred_element_type=f32)
    grad_router = jnp.sum(grad_router.reshape(width, 3, experts), axis=1)
    dmiddle_part, grad_gain_ffn = rms_grad(middle, inverse_m, gain_ffn, dnormed)
    dmiddle = cot + dmiddle_part
    dattn = dmiddle.astype(bf16)
    grad_out = lax.dot_general(heads_out, dattn, (((0,), (0,)), ((), ())), preferred_element_type=f32)
    dheads = lax.dot_general(dattn, out_full, (((1,), (1,)), ((), ())), preferred_element_type=f32).astype(bf16)

    produced = jnp.dot(active.reshape(-1, active.shape[2]), w_down, preferred_element_type=f32)
    produced = produced.astype(bf16).reshape(-1, padded, width)
    back = lax.all_to_all(produced, ("expert", "team"), split_axis=0, concat_axis=0, tiled=True)
    dheads, sum_down = lax.optimization_barrier((dheads, sum_down))
    sum_down = lax.all_to_all(sum_down, "team", split_axis=0, concat_axis=0, tiled=True)

    dqkv, drel = attend_grad(own_list, table, qkv, heads_out, dheads, lse, n_prompt, n_cont, group, head_size)
    grad_qkv = jnp.einsum("rd,cre->cde", normed, dqkv, preferred_element_type=f32).astype(bf16)
    drel = drel.reshape(head_count, -1)[:, prompt_len:]
    grad_rel = jnp.einsum("bt,ht->bh", bucket_hot, drel, precision=lax.Precision.HIGHEST)

    rel_column = jnp.pad(grad_rel.reshape(fsdp, rel_rows), ((0, 0), (0, shard - rel_rows))).reshape(width, 1)
    small = [grad_router, grad_gain_ffn[:, None], rel_column, jnp.zeros((width, 128 - experts - 2), f32)]
    small = jnp.concatenate(small, axis=1).astype(bf16)
    small, sum_down = lax.optimization_barrier((small, sum_down))
    sum_qkv, sum_out, small, sum_in, dx, mixed_out = finish(
        (grad_qkv, grad_out.astype(bf16)[None], small[None]),
        sum_in,
        jnp.broadcast_to(gain_attn[None], (8, width)),
        target,
        gate_rows,
        dqkv,
        qkv_full,
        x_low,
        dmiddle,
        middle,
        back,
        n_prompt,
        units,
        padded,
        cycle,
        group,
    )
    return (
        mixed_out[:n_prompt][None],
        mixed_out[n_prompt:][None, None],
        dx[:n_prompt][None],
        dx[n_prompt:][None, None],
        jnp.sum(sum_qkv * w_qkv.astype(f32), axis=1) / norm_attn.astype(f32),
        small[:, experts],
        sum_qkv,
        sum_out,
        small[:rel_rows, experts + 1].reshape(-1, head_count),
        small[:, :experts],
        sum_in.astype(f32),
        sum_down.astype(f32),
    )


def ring_of_chips(mesh):
    devices = mesh.devices[:, 0]
    chips = len(devices) // 2
    across = [getattr(d, "coords", None) for d in devices[::2]]
    if any(c is None for c in across):
        return list(range(chips))
    columns = len({tuple(c)[0] for c in across})
    levels = chips // columns
    if columns < 2 or levels % 2 or levels * columns != chips:
        return list(range(chips))
    cycle = [0]
    for z in range(levels):
        row = list(range(1, columns))
        cycle += [z * columns + i for i in (row if z % 2 == 0 else row[::-1])]
    return cycle + [z * columns for z in range(levels - 1, 0, -1)]


def solution(mesh):
    fsdp, group = mesh.devices.shape
    cycle = ring_of_chips(mesh)
    mesh = jax.sharding.Mesh(mesh.devices.reshape(fsdp // 4, 4, group), ("depth", "team", "expert"))
    rows = ("depth", "team")
    in_specs = (
        P(rows, "expert", None),
        P(rows, "expert", None, None),
        P(rows, "expert", None),
        P(rows, "expert", None, None),
        P(rows, "expert", None),
        P(rows, "expert", None, None),
        P(),
        P(rows),
        P(rows),
        P(rows, None),
        P(rows, None),
        P(rows, None),
        P(rows, None),
        P("expert", rows, None),
        P("expert", rows, None),
    )
    out_specs = (
        P(rows, "expert", None),
        P(rows, "expert", None, None),
        P(rows, "expert", None),
        P(rows, "expert", None, None),
        P(rows),
        P(rows),
        P(rows, None),
        P(rows, None),
        P(rows, None),
        P(rows, None),
        P("expert", rows, None),
        P("expert", rows, None),
    )
    return jax.shard_map(
        functools.partial(per_device, cycle),
        mesh=mesh,
        in_specs=in_specs,
        out_specs=out_specs,
        check_vma=False,
    )
```

```python
import functools

import jax
import jax.numpy as jnp
from jax import lax
from jax.experimental import pallas as pl
from jax.experimental.pallas import tpu as pltpu
from jax.sharding import PartitionSpec as P

epsilon = 1e-06
blocked = -1e30
f32 = jnp.float32
bf16 = jnp.bfloat16
KB = 128
VMEM_LIMIT = 60 * 1024 * 1024


def nn(a, b):
    return lax.dot_general(a, b, (((1,), (0,)), ((), ())), preferred_element_type=f32)


def nt(a, b):
    return lax.dot_general(a, b, (((1,), (1,)), ((), ())), preferred_element_type=f32)


def tn(a, b):
    return lax.dot_general(a, b, (((0,), (0,)), ((), ())), preferred_element_type=f32)


def make_strips(table_ref, strip_ref):
    width = strip_ref.shape[2]
    for h in range(2):
        wide = jnp.broadcast_to(table_ref[0, h : h + 1, :], (KB, width))
        strip_ref[h] = pltpu.roll(wide, 0, 1, stride=1, stride_axis=0)


def query_sets(own, n_prompt, n_cont, group, most):
    prompt_len = group * n_prompt
    rows = n_prompt + n_cont
    place = [lax.rem(own + s, group) * n_prompt for s in range(group)]
    start = [0] + [rows + s * n_prompt for s in range(group - 1)]
    sets = []
    for base, count, first_place in ((0, n_prompt, place[0]), (n_prompt, n_cont, prompt_len)):
        size = most if count % most == 0 else count
        for first in range(0, count, size):
            keys = [(base, first + size, prompt_len + first)]
            for s in range(group):
                if base or s:
                    keys.append((start[s], n_prompt, prompt_len + first_place + first - place[s]))
            sets.append((base + first, size, keys))
    return sets


def strip_window(strip_ref, h, offset, keys, rows):
    parts = []
    for kb in range(keys // KB):
        start = offset - kb * KB
        if not isinstance(start, int):
            start = pl.multiple_of(start, KB)
        parts.append(strip_ref[h, :, pl.ds(start, rows)])
    return parts[0] if len(parts) == 1 else jnp.concatenate(parts, axis=0)


def head_lanes(x, h, head_size, other=0.0):
    lanes = lax.broadcasted_iota(jnp.int32, x.shape, 1)
    return jnp.where((lanes >= h * head_size) & (lanes < (h + 1) * head_size), x, jnp.full_like(x, other))


def attend_kernel(n_prompt, n_cont, group, head_size, own_ref, table_ref, q_ref, k_ref, v_ref, o_ref, lse_ref, strip_ref):
    make_strips(table_ref, strip_ref)
    scale = jnp.asarray(head_size**-0.5, bf16)
    for first, rows, keys in query_sets(own_ref[0], n_prompt, n_cont, group, 512):
        q_pair = q_ref[first : first + rows, :] * scale
        heads = []
        for h in range(2):
            q = head_lanes(q_pair, h, head_size)
            m = l = acc = None
            for start, count, offset in keys:
                s = nt(k_ref[start : start + count, :], q) + strip_window(strip_ref, h, offset, count, rows)
                top = jnp.max(s, axis=0, keepdims=True)
                m_new = top if m is None else jnp.maximum(m, top)
                p = jnp.exp(s - m_new)
                both = tn(head_lanes(v_ref[start : start + count, :], h, head_size, 1.0), p.astype(bf16))
                out = both[h * head_size : (h + 1) * head_size]
                total = both[(1 - h) * head_size : (1 - h) * head_size + 1]
                if m is None:
                    l, acc = total, out
                else:
                    shrink = jnp.exp(m - m_new)
                    l, acc = l * shrink + total, acc * shrink + out
                m = m_new
            heads.append(acc / l)
            lse_ref[0, h : h + 1, first : first + rows] = m + jnp.log(l)
        o_ref[first : first + rows, :] = jnp.concatenate(heads, axis=0).T.astype(bf16)


def spare_lanes(row, h, head_size):
    terms, left = [], -row
    for _ in range(3):
        terms.append(left.astype(bf16).astype(f32))
        left = left - terms[-1]
    terms.append(jnp.zeros((5, row.shape[1]), f32))
    before = (1 - h) * head_size
    if before:
        terms = [jnp.zeros((before, row.shape[1]), f32)] + terms
    terms.append(jnp.zeros((2 * head_size - before - 8, row.shape[1]), f32))
    return jnp.concatenate(terms, axis=0).T.astype(bf16)


def spare_ones(x, h, head_size):
    lanes = lax.broadcasted_iota(jnp.int32, x.shape, 1) - (1 - h) * head_size
    return jnp.where((lanes >= 0) & (lanes < 3), jnp.ones_like(x), x)


def attend_grad_kernel(n_prompt, n_cont, group, head_size, own_ref, table_ref, q_ref, k_ref, v_ref, o_ref, do_ref, lse_ref,
                       dqkv_ref, drel_ref, strip_ref, diag_ref, dk_ref, dv_ref):
    make_strips(table_ref, strip_ref)
    width = strip_ref.shape[2]
    mine = n_prompt + n_cont
    scale = jnp.asarray(head_size**-0.5, bf16)
    diag_ref[...] = jnp.zeros_like(diag_ref)
    dk_ref[...] = jnp.zeros_like(dk_ref)
    dv_ref[...] = jnp.zeros_like(dv_ref)
    for first, rows, keys in query_sets(own_ref[0], n_prompt, n_cont, group, 256):
        q_pair = q_ref[first : first + rows, :] * scale
        do_pair = do_ref[first : first + rows, :]
        inner = (do_pair.astype(f32) * o_ref[first : first + rows, :].astype(f32)).T
        heads = []
        for h in range(2):
            q = head_lanes(q_pair, h, head_size)
            do = head_lanes(do_pair, h, head_size)
            delta = jnp.sum(inner[h * head_size : (h + 1) * head_size], axis=0, keepdims=True)
            q_less = q + spare_lanes(lse_ref[0, h : h + 1, first : first + rows], h, head_size)
            do_less = do + spare_lanes(delta, h, head_size)
            dq = None
            for start, count, offset in keys:
                at = slice(start, start + count)
                k = k_ref[at, :]
                p = jnp.exp(nt(spare_ones(k, h, head_size), q_less) + strip_window(strip_ref, h, offset, count, rows))
                ds = p * nt(spare_ones(v_ref[at, :], h, head_size), do_less)
                for kb in range(count // KB):
                    lane = offset - kb * KB
                    if not isinstance(lane, int):
                        lane = pl.multiple_of(lane, KB)
                    diag_ref[h, :, pl.ds(lane, rows)] += ds[kb * KB : (kb + 1) * KB]
                ds = ds.astype(bf16)
                dv_ref[at, :] += nn(p.astype(bf16), do)
                dk_ref[at, :] += nn(ds, q)
                part = tn(k, ds)[h * head_size : (h + 1) * head_size]
                dq = part if dq is None else dq + part
            heads.append(dq)
        dqkv_ref[0, first : first + rows, :] = (jnp.concatenate(heads, axis=0).T * (head_size**-0.5)).astype(bf16)
    if dqkv_ref.shape[1] > mine:
        dqkv_ref[0, mine:, :] = jnp.zeros((dqkv_ref.shape[1] - mine, dqkv_ref.shape[2]), bf16)
    dqkv_ref[1] = dk_ref[...].astype(bf16)
    dqkv_ref[2] = dv_ref[...].astype(bf16)
    for h in range(2):
        x = diag_ref[h]
        half = KB // 2
        while half >= 8:
            x = x[:half] + pltpu.roll(x[half:], width - half, 1)
            half //= 2
        row = x[0:1]
        for i in range(1, 8):
            row = row + pltpu.roll(x[i : i + 1], width - i, 1)
        drel_ref[0, h : h + 1, :] = row


def attention_specs(rows, width, pairs):
    return [
        pl.BlockSpec((1, 2, width), lambda j, own: (j, 0, 0)),
        pl.BlockSpec((rows, 128), lambda j, own: (0, j)),
        pl.BlockSpec((rows, 128), lambda j, own: (0, pairs + j)),
        pl.BlockSpec((rows, 128), lambda j, own: (0, 2 * pairs + j)),
    ]


def attend(own, table, qkv, n_prompt, n_cont, group, head_size):
    pairs, _, width = table.shape
    mine = n_prompt + n_cont
    work = pairs * 2 * (n_prompt * n_prompt * group + n_cont * (n_prompt * group + n_cont))
    return pl.pallas_call(
        functools.partial(attend_kernel, n_prompt, n_cont, group, head_size),
        out_shape=(
            jax.ShapeDtypeStruct((mine, pairs * 128), bf16),
            jax.ShapeDtypeStruct((pairs, 2, mine), f32),
        ),
        grid_spec=pltpu.PrefetchScalarGridSpec(
            num_scalar_prefetch=1,
            grid=(pairs,),
            in_specs=attention_specs(qkv.shape[0], width, pairs),
            out_specs=(
                pl.BlockSpec((mine, 128), lambda j, own: (0, j)),
                pl.BlockSpec((1, 2, mine), lambda j, own: (j, 0, 0)),
            ),
            scratch_shapes=[pltpu.VMEM((2, KB, width), f32)],
        ),
        compiler_params=pltpu.CompilerParams(vmem_limit_bytes=VMEM_LIMIT),
        cost_estimate=pl.CostEstimate(flops=16 * work * head_size, bytes_accessed=16 * mine * pairs * 128, transcendentals=work),
        name="attend",
    )(own, table, qkv, qkv, qkv)


def attend_grad(own, table, qkv, heads_out, dheads, lse, n_prompt, n_cont, group, head_size):
    pairs, _, width = table.shape
    rows, mine = qkv.shape[0], n_prompt + n_cont
    work = pairs * 2 * (n_prompt * n_prompt * group + n_cont * (n_prompt * group + n_cont))
    return pl.pallas_call(
        functools.partial(attend_grad_kernel, n_prompt, n_cont, group, head_size),
        out_shape=(
            jax.ShapeDtypeStruct((3, rows, pairs * 128), bf16),
            jax.ShapeDtypeStruct((pairs, 2, width), f32),
        ),
        grid_spec=pltpu.PrefetchScalarGridSpec(
            num_scalar_prefetch=1,
            grid=(pairs,),
            in_specs=attention_specs(rows, width, pairs)
            + [
                pl.BlockSpec((mine, 128), lambda j, own: (0, j)),
                pl.BlockSpec((mine, 128), lambda j, own: (0, j)),
                pl.BlockSpec((1, 2, mine), lambda j, own: (j, 0, 0)),
            ],
            out_specs=(
                pl.BlockSpec((3, rows, 128), lambda j, own: (0, 0, j)),
                pl.BlockSpec((1, 2, width), lambda j, own: (j, 0, 0)),
            ),
            scratch_shapes=[
                pltpu.VMEM((2, KB, width), f32),
                pltpu.VMEM((2, KB, width), f32),
                pltpu.VMEM((rows, 128), f32),
                pltpu.VMEM((rows, 128), f32),
            ],
        ),
        compiler_params=pltpu.CompilerParams(vmem_limit_bytes=VMEM_LIMIT),
        cost_estimate=pl.CostEstimate(flops=40 * work * head_size, bytes_accessed=40 * mine * pairs * 128, transcendentals=work),
        name="attend_grad",
    )(own, table, qkv, qkv, qkv, heads_out, dheads, lse)


def unit_list(n_prompt, n_cont, cap_prompt, cap_cont, padded):
    if cap_prompt % 16 == 0 and cap_cont % 16 == 0:
        return ((0, n_prompt, 0, cap_prompt), (n_prompt, n_cont, cap_prompt, cap_cont))
    return ((0, n_prompt + n_cont, 0, padded),)


def slots_of(units, routes_ref, experts, padded, caps):
    found = []
    for (first, rows, slot), cap in zip(units, caps):
        numbers = lax.broadcasted_iota(jnp.int32, (experts, rows), 0)
        routes = [routes_ref[c : c + 1, first : first + rows] for c in range(2)]
        hits = [numbers == r for r in routes]
        both = jnp.where(hits[0] | hits[1], 1.0, 0.0).astype(bf16)
        before = lax.broadcasted_iota(jnp.int32, (rows, rows), 0) < lax.broadcasted_iota(jnp.int32, (rows, rows), 1)
        earlier = nn(both, jnp.where(before, 1.0, 0.0).astype(bf16))
        for c in range(2):
            count = jnp.sum(jnp.where(hits[c], earlier, 0.0), axis=0, keepdims=True).astype(jnp.int32)
            found.append(jnp.where(count < cap, routes[c] * padded + slot + count, -1))
    return found


def chosen_rows(target_ref, unit, experts, padded):
    first, rows, slot, slots = unit
    parts = []
    for e in range(experts):
        numbers = lax.broadcasted_iota(jnp.int32, (slots, rows), 0) + (e * padded + slot)
        hit = [numbers == target_ref[c : c + 1, first : first + rows] for c in range(2)]
        parts.append(jnp.where(hit[0] | hit[1], 1.0, 0.0).astype(bf16))
    return jnp.concatenate(parts, axis=0)


def target_columns(target_ref, unit):
    first, rows = unit[:2]
    turned = target_ref[:, first : first + rows].astype(f32).T.astype(jnp.int32)
    return [turned[:, c : c + 1] for c in range(2)]


def cots_kernel(units, caps, experts, padded, routes_ref, cot_refs, target_ref, out_ref):
    first_slot = 0
    row_units = []
    first = 0
    for rows, cap in caps:
        row_units.append((first, rows, first_slot))
        first, first_slot = first + rows, first_slot + cap
    found = slots_of(row_units, routes_ref, experts, padded, [cap for _, cap in caps])
    target_ref[...] = jnp.full(target_ref.shape, -1, jnp.int32)
    for u, (first, rows, _) in enumerate(row_units):
        for c in range(2):
            target_ref[c : c + 1, first : first + rows] = found[2 * u + c]
    for unit in units:
        first, rows, slot, slots = unit
        cot = jnp.concatenate([ref[...] for ref in cot_refs], axis=0) if len(units) == 1 else cot_refs[1 if first else 0][...]
        got = nn(chosen_rows(target_ref, unit, experts, padded), cot).astype(bf16)
        for e in range(experts):
            out_ref[e, slot : slot + slots, :] = got[e * slots : (e + 1) * slots]


def remote(src, dst, device, send_sem, recv_sem):
    return pltpu.make_async_remote_copy(
        src_ref=src, dst_ref=dst, send_sem=send_sem, recv_sem=recv_sem, device_id=device, device_id_type=pl.DeviceIdType.MESH
    )


def greet(devices):
    barrier = pltpu.get_barrier_semaphore()
    for device in devices:
        pl.semaphore_signal(barrier, inc=1, device_id=device, device_id_type=pl.DeviceIdType.MESH)
    pl.semaphore_wait(barrier, len(devices))


def look_up(table, i):
    found = jnp.int32(table[0])
    for j in range(1, len(table)):
        found = jnp.where(i == j, jnp.int32(table[j]), found)
    return found


def ring_places(cycle):
    count = len(cycle)
    inverse = [0] * count
    for p, c in enumerate(cycle):
        inverse[c] = p
    team = lax.axis_index("team")
    place = look_up(inverse, lax.axis_index("depth") * 2 + team // 2)

    def chip(distance):
        return look_up(cycle, lax.rem(place + (distance + count), count))

    def device(chip, core):
        return {"depth": chip // 2, "team": lax.rem(chip, 2) * 2 + core}

    return chip, device, lax.rem(team, 2)


def ring_pieces(cut, qkv, wout, extra):
    return ((qkv, slice(0, cut), 0), (qkv, slice(cut, qkv.shape[-1]), 1), (wout, slice(0, wout.shape[-1]), 1), (extra, slice(0, extra.shape[-1]), 1))


def ring_gather(cycle, cut, hops_from, hops_to, shards, outs, sems, between=()):
    ring_send, ring_recv, core_send, core_recv = sems
    count = len(cycle)
    chip, at, core = ring_places(cycle)
    right, left, partner = at(chip(1), core), at(chip(-1), core), {"team": lax.axis_index("team") + 1 - 2 * core}
    pieces = ring_pieces(cut, *outs)
    long, short = count // 2, count - 1 - count // 2
    streams = ((0, right, -1, long), (1, left, 1, long), (0, left, 1, short), (1, right, -1, short))
    started, arrivals = [], []

    def start(copy):
        copy.start()
        started.append(copy)

    def slot(p, c, k):
        return pieces[p][0].at[c, k, :, pieces[p][1]]

    def source(p, c):
        return slot(p, c, core) if shards is None else ring_pieces(cut, *shards)[p][0].at[:, pieces[p][1]]

    def hop_copies(k, c, hop, first=False):
        half, device = streams[k][:2]
        return [
            remote(source(p, c) if first else slot(p, c, core), slot(p, c, core), device, ring_send.at[k, hop, p], ring_recv.at[k, hop, p])
            for p in range(len(pieces))
            if pieces[p][2] == half
        ]

    def across(c, half, first=False):
        for p in range(len(pieces)):
            if pieces[p][2] == half:
                number = len(arrivals)
                start(remote(source(p, c) if first else slot(p, c, core), slot(p, c, core), partner, core_send.at[number], core_recv.at[number]))
                arrivals.append(slot(p, c, 1 - core))

    for k, (half, device, sign, hops) in enumerate(streams):
        if hops_from < hops:
            for copy in hop_copies(k, chip(sign * hops_from), hops_from, hops_from == 0):
                start(copy)
    if hops_from == 0:
        for half in range(2):
            across(chip(0), half, True)
    for action in between:
        action()
    for hop in range(hops_from, hops_to):
        for k, (half, device, sign, hops) in enumerate(streams):
            if hop < hops:
                other = chip(sign * (1 + hop))
                for copy in hop_copies(k, other, hop):
                    copy.wait_recv()
                if hop + 1 < min(hops, hops_to):
                    for copy in hop_copies(k, other, hop + 1):
                        start(copy)
                across(other, half)
    waits = [remote(v, v, partner, core_send.at[n], core_recv.at[n]).wait_recv for n, v in enumerate(arrivals)]
    return waits + [copy.wait_send for copy in started]


def ring_neighbours(cycle):
    chip, at, core = ring_places(cycle)
    return [at(chip(1), core), at(chip(-1), core), {"team": lax.axis_index("team") + 1 - 2 * core}]


def front_kernel(cycle, cut, hops, qkv_ref, wout_ref, extra_ref, win_ref, qkv_out, wout_out, extra_out, win_out,
                 ring_send, ring_recv, core_send, core_recv, team_send, team_recv, local_sem):
    chip, _, core = ring_places(cycle)
    team = lax.axis_index("team")
    mates = [team + d - 4 * ((team + d) // 4) for d in range(1, 4)]
    greet(ring_neighbours(cycle) + [{"team": t} for t in mates])
    waits = []

    def swap():
        for d, t in enumerate(mates):
            copy = remote(win_ref.at[t], win_out.at[team], {"team": t}, team_send.at[d], team_recv.at[d])
            copy.start()
            source = team + 3 - d - 4 * ((team + 3 - d) // 4)
            waits.append(remote(win_ref.at[t], win_out.at[source], {"team": t}, team_send.at[d], team_recv.at[d]).wait_recv)
            waits.append(copy.wait_send)
        keep = [(win_ref.at[team], win_out.at[team])]
        keep += [(src, out.at[chip(0), core]) for src, out in ((qkv_ref, qkv_out), (wout_ref, wout_out), (extra_ref, extra_out))]
        for p, (src, dst) in enumerate(keep):
            copy = pltpu.make_async_copy(src, dst, local_sem.at[p])
            copy.start()
            waits.append(copy.wait)

    outs = (qkv_out, wout_out, extra_out)
    sems = (ring_send, ring_recv, core_send, core_recv)
    waits += ring_gather(cycle, cut, 0, hops, (qkv_ref, wout_ref, extra_ref), outs, sems, (swap,))
    for wait in waits:
        wait()


def front_rest_kernel(cycle, group, fixed, cut, hops, qkv_in, wout_in, extra_in, wdown_ref, x_ref, routes_ref, prompt_cot_ref,
                      cont_cot_ref, qkv_out, wout_out, extra_out, wdown_out, x_out, target_ref, cots_ref,
                      ring_send, ring_recv, core_send, core_recv, row_send, row_recv, team_send, team_recv, local_sem):
    own, team = lax.axis_index("expert"), lax.axis_index("team")
    rows = [lax.rem(own + s, group) for s in range(1, group)]
    mates = [team + d - 4 * ((team + d) // 4) for d in range(1, 4)]
    greet(ring_neighbours(cycle) + [{"expert": g} for g in rows] + [{"team": t} for t in mates])
    waits = []

    def others():
        for d, t in enumerate(mates):
            copy = remote(wdown_ref.at[t], wdown_out.at[team], {"team": t}, team_send.at[d], team_recv.at[d])
            copy.start()
            source = team + 3 - d - 4 * ((team + 3 - d) // 4)
            waits.append(remote(wdown_ref.at[t], wdown_out.at[source], {"team": t}, team_send.at[d], team_recv.at[d]).wait_recv)
            waits.append(copy.wait_send)
        copy = pltpu.make_async_copy(wdown_ref.at[team], wdown_out.at[team], local_sem)
        copy.start()
        waits.append(copy.wait)
        for s, g in enumerate(rows):
            back = lax.rem(own + group - (s + 1), group)
            copy = remote(x_ref, x_out.at[s], {"expert": back}, row_send.at[s], row_recv.at[s])
            copy.start()
            waits.append(remote(x_ref, x_out.at[s], {"expert": g}, row_send.at[s], row_recv.at[s]).wait_recv)
            waits.append(copy.wait_send)
        cots_kernel(*fixed, routes_ref, (prompt_cot_ref, cont_cot_ref), target_ref, cots_ref)

    outs = (qkv_out, wout_out, extra_out)
    sems = (ring_send, ring_recv, core_send, core_recv)
    waits += ring_gather(cycle, cut, hops, len(cycle) // 2, None, outs, sems, (others,))
    for wait in waits:
        wait()


def front(w_qkv, w_out, extra, expert_in, expert_out, x_prompt, routes, prompt_cot, cont_cot, fixed, cycle, group):
    count = len(cycle)
    experts, padded = fixed[2:]
    rows, columns = w_qkv.shape
    cut = (columns + w_out.shape[1] + extra.shape[1]) // 256 * 128
    hops = max(1, count // 8)
    anywhere, vmem = pl.BlockSpec(memory_space=pl.ANY), pl.BlockSpec(memory_space=pltpu.VMEM)
    ring_sems = [pltpu.SemaphoreType.DMA((4, count, 4))] * 2 + [pltpu.SemaphoreType.DMA((4 * count,))] * 2
    dense_shapes = tuple(jax.ShapeDtypeStruct((count, 2) + v.shape, bf16) for v in (w_qkv, w_out, extra))
    cost = pl.CostEstimate(flops=10**10, bytes_accessed=10**8, transcendentals=0)
    *dense, w_in = pl.pallas_call(
        functools.partial(front_kernel, cycle, cut, hops),
        out_shape=dense_shapes + (jax.ShapeDtypeStruct(expert_in.shape, bf16),),
        in_specs=[anywhere] * 4,
        out_specs=(anywhere,) * 4,
        scratch_shapes=ring_sems + [pltpu.SemaphoreType.DMA((3,))] * 2 + [pltpu.SemaphoreType.DMA((4,))],
        compiler_params=pltpu.CompilerParams(collective_id=0, has_side_effects=True, vmem_limit_bytes=VMEM_LIMIT),
        cost_estimate=cost,
        name="front",
    )(w_qkv, w_out, extra, expert_in)
    results = pl.pallas_call(
        functools.partial(front_rest_kernel, cycle, group, fixed, cut, hops),
        out_shape=dense_shapes
        + (
            jax.ShapeDtypeStruct(expert_out.shape, bf16),
            jax.ShapeDtypeStruct((group - 1,) + x_prompt.shape, bf16),
            jax.ShapeDtypeStruct(routes.shape, jnp.int32),
            jax.ShapeDtypeStruct((experts, padded, prompt_cot.shape[1]), bf16),
        ),
        in_specs=[anywhere] * 5 + [vmem] * 3,
        out_specs=(anywhere,) * 5 + (vmem,) * 2,
        scratch_shapes=ring_sems
        + [pltpu.SemaphoreType.DMA((group,))] * 2
        + [pltpu.SemaphoreType.DMA((3,))] * 2
        + [pltpu.SemaphoreType.DMA],
        input_output_aliases={0: 0, 1: 1, 2: 2},
        compiler_params=pltpu.CompilerParams(collective_id=4, has_side_effects=True, vmem_limit_bytes=VMEM_LIMIT),
        cost_estimate=cost,
        name="front_rest",
    )(*dense, expert_out, x_prompt, routes, prompt_cot, cont_cot)
    return [v.reshape(count * 2 * rows, v.shape[3]) for v in results[:3]] + [w_in] + list(results[3:])


def team_ring(group):
    team, own = lax.axis_index("team"), lax.axis_index("expert")

    def peer(i):
        g, t = lax.rem(own + i // 4, group), lax.rem(team + lax.rem(i, 4), 4)
        return g * 4 + t, {"team": t, "expert": g}

    def back_from(i):
        return lax.rem(own + (group - i // 4), group) * 4 + lax.rem(team + (4 - lax.rem(i, 4)), 4)

    return own * 4 + team, peer, back_from


def expert_up_kernel(units, group, experts, padded, target_ref, gate_ref, routes_ref, z_ref, cots_ref, w_in_ref,
                     active_hbm, slope_hbm, grad_hbm, dproduced_ref, arrived_t_ref,
                     stage_ref, gate_stage, arrived_ref, gate_in, held_ref, chunk_ref, dproduced_t_ref, tile_ref, row_send, row_recv, gate_send, gate_recv, held_sem, chunk_sem, tile_sem):
    me, peer, back_from = team_ring(group)
    sources = 4 * group
    hidden = w_in_ref.shape[1]
    step = next(n for n in (512, 256, 128) if hidden % n == 0)
    greet([peer(jnp.int32(i))[1] for i in range(1, sources)])
    for unit in units:
        first, rows, slot, slots = unit
        chosen = chosen_rows(target_ref, unit, experts, padded)
        got = nn(chosen, z_ref[first : first + rows, :]).astype(bf16)
        features = []
        for c in range(2):
            left = gate_ref[c : c + 1, first : first + rows]
            for _ in range(3):
                low = left.astype(bf16).astype(f32)
                features.append(low)
                left = left - low
        features.append(routes_ref[0:1, first : first + rows].astype(f32))
        features.append(jnp.zeros_like(features[0]))
        picked = nt(jnp.concatenate(features, axis=0).astype(bf16), chosen)
        gates = [picked[3 * c : 3 * c + 1] + picked[3 * c + 1 : 3 * c + 2] + picked[3 * c + 2 : 3 * c + 3] for c in range(2)]
        for e in range(experts):
            part = slice(e * slots, (e + 1) * slots)
            stage_ref[e, slot : slot + slots, :] = got[part]
            gate = jnp.where(picked[6:7, part] == float(e), gates[0][:, part], gates[1][:, part])
            gate_stage[e, :, slot : slot + slots] = jnp.broadcast_to(gate, (8, slots))

    def sends(i, to):
        number, device = peer(i)
        return (
            remote(gate_stage.at[number], gate_in.at[to], device, gate_send.at[i], gate_recv.at[i]),
            remote(stage_ref.at[number], arrived_ref.at[to], device, row_send.at[i], row_recv.at[i]),
        )

    for i in range(1, sources):
        for copy in sends(jnp.int32(i), me):
            copy.start()
    arrived_ref[me] = stage_ref[me]
    gate_in[me] = gate_stage[me]

    def keep(number, slot):
        return pltpu.make_async_copy(chunk_ref.at[slot], slope_hbm.at[number], chunk_sem.at[slot])

    def out(number):
        return pltpu.make_async_copy(held_ref.at[number], active_hbm.at[number], held_sem.at[number])

    def source(i, carry):
        number, slot = back_from(i), lax.rem(i, 2)

        @pl.when(i > 0)
        def _():
            for copy in sends(i, number):
                copy.wait_recv()

        @pl.when(i >= 2)
        def _():
            keep(back_from(i - 2), slot).wait()

        dproduced_ref[number] = (cots_ref[number].astype(f32) * gate_in[number].T[:, 0:1]).astype(bf16)
        arrived = arrived_ref[number]
        for first in range(0, hidden, step):
            at = slice(first, first + step)
            active, slope = gelu_parts(nn(arrived, w_in_ref[:, at]))
            chunk_ref[slot, :, at] = slope.astype(bf16)
            held_ref[number, :, at] = active.astype(bf16)
        keep(number, slot).start()
        out(number).start()
        return carry

    lax.fori_loop(0, sources, source, 0)
    width = dproduced_ref.shape[2]
    dproduced_t_ref[...] = dproduced_ref[...].reshape(-1, width).T
    arrived_t_ref[...] = arrived_ref[...].reshape(-1, width).T

    def put(f):
        at = pl.ds(pl.multiple_of(f * step, step), step)
        return pltpu.make_async_copy(tile_ref.at[lax.rem(f, 2)], grad_hbm.at[at, :], tile_sem.at[lax.rem(f, 2)])

    def product(f, carry):
        @pl.when(f >= 2)
        def _():
            put(f - 2).wait()

        active = held_ref[:, :, pl.ds(pl.multiple_of(f * step, step), step)].reshape(-1, step)
        tile_ref[lax.rem(f, 2)] = nn(dproduced_t_ref[...], active).astype(bf16).T
        put(f).start()
        return carry

    steps = hidden // step
    lax.fori_loop(0, steps, product, 0)
    for f in range(max(0, steps - 2), steps):
        put(jnp.int32(f)).wait()
    for i in range(sources - 2, sources):
        keep(back_from(jnp.int32(i)), jnp.int32(i % 2)).wait()
    for i in range(sources):
        out(back_from(jnp.int32(i))).wait()
    for i in range(1, sources):
        for copy in sends(jnp.int32(i), me):
            copy.wait_send()


def expert_up(target, gates, routes, z, cots, w_in, units, group, experts, padded):
    sources = 4 * group
    width, hidden = w_in.shape
    step = next(n for n in (512, 256, 128) if hidden % n == 0)
    slots = sources * padded
    anywhere, vmem = pl.BlockSpec(memory_space=pl.ANY), pl.BlockSpec(memory_space=pltpu.VMEM)
    return pl.pallas_call(
        functools.partial(expert_up_kernel, units, group, experts, padded),
        out_shape=(
            jax.ShapeDtypeStruct((sources, padded, hidden), bf16),
            jax.ShapeDtypeStruct((sources, padded, hidden), bf16),
            jax.ShapeDtypeStruct((hidden, width), bf16),
            jax.ShapeDtypeStruct((sources, padded, width), bf16),
            jax.ShapeDtypeStruct((width, slots), bf16),
        ),
        in_specs=[vmem] * 6,
        out_specs=(anywhere,) * 3 + (vmem,) * 2,
        scratch_shapes=[
            pltpu.VMEM((experts, padded, width), bf16),
            pltpu.VMEM((experts, 8, padded), f32),
            pltpu.VMEM((sources, padded, width), bf16),
            pltpu.VMEM((sources, 8, padded), f32),
            pltpu.VMEM((sources, padded, hidden), bf16),
            pltpu.VMEM((2, padded, hidden), bf16),
            pltpu.VMEM((width, slots), bf16),
            pltpu.VMEM((2, step, width), bf16),
        ]
        + [pltpu.SemaphoreType.DMA((sources,))] * 5
        + [pltpu.SemaphoreType.DMA((2,))] * 2,
        compiler_params=pltpu.CompilerParams(collective_id=1, has_side_effects=True, vmem_limit_bytes=VMEM_LIMIT),
        cost_estimate=pl.CostEstimate(flops=6 * slots * width * hidden, bytes_accessed=10**8, transcendentals=0),
        name="expert_up",
    )(target, gates, routes, z, cots, w_in)


def expert_back_kernel(units, group, experts, padded, target_ref, dproduced_hbm, slope_hbm, active_hbm, arrived_t_ref, w_in_ref, w_down_ref,
                       grad_hbm, dz_ref, inner_ref, dbefore_ref, stage_ref, back_ref, inner_stage, inner_back, tile_ref,
                       active_ref, copy_sem, active_sem, tile_sem, row_send, row_recv, inner_send, inner_recv):
    me, peer, back_from = team_ring(group)
    sources = 4 * group
    hidden = w_in_ref.shape[1]
    tile = next(t for t in (512, 256) if hidden % t == 0)

    def load(i):
        number = peer(i)[0]
        return (
            pltpu.make_async_copy(slope_hbm.at[number], dbefore_ref.at[number], copy_sem.at[0, i]),
            pltpu.make_async_copy(dproduced_hbm.at[number], stage_ref.at[number], copy_sem.at[1, i]),
        )

    def sends(i, to):
        number, device = peer(i)
        return (
            remote(inner_stage.at[number], inner_back.at[to], device, inner_send.at[i], inner_recv.at[i]),
            remote(stage_ref.at[number], back_ref.at[to], device, row_send.at[i], row_recv.at[i]),
        )

    turns = sources // 2

    def pair(turn):
        return 2 * turn + 1, lax.rem(2 * turn + 2, sources)

    def fetch(turn):
        return [
            pltpu.make_async_copy(active_hbm.at[peer(i)[0]], active_ref.at[k], active_sem.at[k]) for k, i in enumerate(pair(turn))
        ]

    for i in list(range(1, sources)) + [0]:
        for copy in load(jnp.int32(i)):
            copy.start()
        if i == 2:
            for copy in fetch(jnp.int32(0)):
                copy.start()
    greet([peer(jnp.int32(i))[1] for i in range(1, sources)])

    def source(turn, carry):
        both = pair(turn)
        numbers = [peer(i)[0] for i in both]
        for i in both:
            for copy in load(i):
                copy.wait()
        for copy in fetch(turn):
            copy.wait()
        dproduced = jnp.concatenate([stage_ref[n] for n in numbers], axis=0)
        inner = darrived = None
        for first in range(0, hidden, tile):
            at = slice(first, first + tile)
            dactive = nt(dproduced, w_down_ref[at, :])
            active = active_ref[:, :, at].reshape(2 * padded, tile)
            product = active.astype(f32) * dactive
            for lane in range(0, tile, 128):
                part = product[:, lane : lane + 128]
                inner = part if inner is None else inner + part
            slope = jnp.concatenate([dbefore_ref[n, :, at] for n in numbers], axis=0)
            dbefore = (dactive * slope.astype(f32)).astype(bf16)
            for k, n in enumerate(numbers):
                dbefore_ref[n, :, at] = dbefore[k * padded : (k + 1) * padded]
            part = nt(dbefore, w_in_ref[:, at])
            darrived = part if darrived is None else darrived + part

        @pl.when(turn + 1 < turns)
        def _():
            for copy in fetch(turn + 1):
                copy.start()

        inner = jnp.sum(inner, axis=1, keepdims=True)
        for k, n in enumerate(numbers):
            part = slice(k * padded, (k + 1) * padded)
            inner_stage[n] = jnp.broadcast_to(inner[part], (padded, 128)).T[:8]
            stage_ref[n] = darrived[part].astype(bf16)
        for copy in sends(both[0], me):
            copy.start()

        @pl.when(turn + 1 < turns)
        def _():
            for copy in sends(both[1], me):
                copy.start()

        return carry

    lax.fori_loop(0, turns, source, 0)
    back_ref[me] = stage_ref[me]
    inner_back[me] = inner_stage[me]
    wide = next(n for n in (512, 256, 128) if hidden % n == 0)
    steps = hidden // wide

    def put(f):
        at = pl.ds(pl.multiple_of(f * wide, wide), wide)
        return pltpu.make_async_copy(tile_ref.at[lax.rem(f, 2)], grad_hbm.at[:, at], tile_sem.at[lax.rem(f, 2)])

    def product(f, carry):
        @pl.when(f >= 2)
        def _():
            put(f - 2).wait()

        dbefore = dbefore_ref[:, :, pl.ds(pl.multiple_of(f * wide, wide), wide)].reshape(-1, wide)
        tile_ref[lax.rem(f, 2)] = nn(arrived_t_ref[...], dbefore).astype(bf16)
        put(f).start()
        return carry

    lax.fori_loop(0, steps, product, 0)
    for f in range(max(0, steps - 2), steps):
        put(jnp.int32(f)).wait()
    for i in range(1, sources):
        sends(jnp.int32(i), back_from(jnp.int32(i)))[0].wait_recv()

    def hits(unit, columns, e):
        first, rows, slot, slots = unit
        numbers = lax.broadcasted_iota(jnp.int32, (rows, slots), 1) + (e * padded + slot)
        return [numbers == column for column in columns]

    for unit in units:
        first, rows, slot, slots = unit
        columns = target_columns(target_ref, unit)
        sums = [0.0, 0.0]
        for e in range(experts):
            inner = inner_back[e, 0:1, slot : slot + slots]
            for c, hit in enumerate(hits(unit, columns, e)):
                sums[c] = sums[c] + jnp.sum(jnp.where(hit, inner, 0.0), axis=1, keepdims=True)
        lanes = lax.broadcasted_iota(jnp.int32, (rows, 128), 1)
        both = jnp.where(lanes == 0, sums[0], jnp.where(lanes == 1, sums[1], 0.0))
        inner_ref[:, first : first + rows] = both.T[:8]
    for i in range(1, sources):
        sends(jnp.int32(i), back_from(jnp.int32(i)))[1].wait_recv()
    for unit in units:
        first, rows, slot, slots = unit
        columns = target_columns(target_ref, unit)
        total = None
        for e in range(experts):
            hit = hits(unit, columns, e)
            part = nn(jnp.where(hit[0] | hit[1], 1.0, 0.0).astype(bf16), back_ref[e, slot : slot + slots, :])
            total = part if total is None else total + part
        dz_ref[first : first + rows, :] = total
    for i in range(1, sources):
        for copy in sends(jnp.int32(i), me):
            copy.wait_send()


def expert_back(target, dproduced, slope, active, arrived_t, w_in, w_down, units, group, experts, padded):
    sources, mine = 4 * group, target.shape[1]
    width, hidden = w_in.shape
    anywhere, vmem = pl.BlockSpec(memory_space=pl.ANY), pl.BlockSpec(memory_space=pltpu.VMEM)
    return pl.pallas_call(
        functools.partial(expert_back_kernel, units, group, experts, padded),
        out_shape=(
            jax.ShapeDtypeStruct((width, hidden), bf16),
            jax.ShapeDtypeStruct((mine, width), f32),
            jax.ShapeDtypeStruct((8, mine), f32),
        ),
        in_specs=[vmem, anywhere, anywhere, anywhere] + [vmem] * 3,
        out_specs=(anywhere, vmem, vmem),
        scratch_shapes=[
            pltpu.VMEM((sources, padded, hidden), bf16),
            pltpu.VMEM((sources, padded, width), bf16),
            pltpu.VMEM((experts, padded, width), bf16),
            pltpu.VMEM((sources, 8, padded), f32),
            pltpu.VMEM((experts, 8, padded), f32),
            pltpu.VMEM((2, width, 512 if hidden % 512 == 0 else 256 if hidden % 256 == 0 else 128), bf16),
            pltpu.VMEM((2, padded, hidden), bf16),
            pltpu.SemaphoreType.DMA((2, sources)),
            pltpu.SemaphoreType.DMA((2,)),
            pltpu.SemaphoreType.DMA((2,)),
        ]
        + [pltpu.SemaphoreType.DMA((sources,))] * 4,
        compiler_params=pltpu.CompilerParams(collective_id=2, has_side_effects=True, vmem_limit_bytes=VMEM_LIMIT),
        cost_estimate=pl.CostEstimate(flops=6 * sources * padded * width * hidden, bytes_accessed=10**8, transcendentals=0),
        name="expert_back",
    )(target, dproduced, slope, active, arrived_t, w_in, w_down)


def mix_rows(unit, experts, padded, target_ref, gate_ref, middle_ref, back_ref, out_ref):
    first, rows, slot, slots = unit
    columns = target_columns(target_ref, unit)
    turned = gate_ref[:, first : first + rows].T
    total = middle_ref[first : first + rows, :]
    for e in range(experts):
        numbers = lax.broadcasted_iota(jnp.int32, (rows, slots), 1) + (e * padded + slot)
        weight = sum(jnp.where(numbers == columns[c], turned[:, c : c + 1], 0.0) for c in range(2))
        total = total + nn(weight.astype(bf16), back_ref[e, slot : slot + slots, :])
    out_ref[first : first + rows, :] = total.astype(bf16)


def finish_kernel(cycle, group, n_prompt, units, experts, padded, *refs):
    parts, refs = refs[:3], refs[3:]
    win_ref, gain_ref, target_ref, gate_ref = refs[:4]
    brought, refs = refs[4:10], refs[10:]
    outs, refs = refs[:3], refs[3:]
    win_out, dx_ref, mixed_ref = refs[:3]
    got, send_refs, recv_refs, rows_refs = refs[3:6], refs[6:11], refs[11:16], refs[16:19]
    away_ref, home_ref = refs[19:21]
    held, refs = refs[21:27], refs[27:]
    core_send, core_recv, ring_send, ring_recv, row_send, row_recv, team_send, team_recv, away_send, away_recv, local_sem, bring_sem = refs
    dqkv_ref, w_ref, x_ref, dmiddle_ref, middle_ref, back_ref = held
    sources = list(brought)
    sources[2] = sources[2].at[: x_ref.shape[0], :]
    bring = [pltpu.make_async_copy(src, dst, bring_sem.at[k]) for k, (src, dst) in enumerate(zip(sources, held))]
    for copy in bring:
        copy.start()
    count = len(cycle)
    chip, at, core = ring_places(cycle)
    own, team = lax.axis_index("expert"), lax.axis_index("team")
    right, left, partner = at(chip(1), core), at(chip(-1), core), {"team": team + 1 - 2 * core}
    peers = [{"expert": lax.rem(own + s, group)} for s in range(1, group)]
    mates = [team + d - 4 * ((team + d) // 4) for d in range(1, 4)]
    greet([right, left, partner] + peers + [{"team": t} for t in mates])
    started, ends = [], []

    def start(copy):
        copy.start()
        started.append(copy)

    order = []
    for hop in range(count - 1):
        for distance in (-1 - hop, 1 + hop):
            if (distance + count) % count not in order:
                order.append((distance + count) % count)
    order.append(0)

    def core_copies(number, c):
        return [
            remote(part.at[:, c, 1 - core], got[k].at[c], partner, core_send.at[k, number], core_recv.at[k, number])
            for k, part in enumerate(parts)
        ]

    for number, distance in enumerate(order):
        for copy in core_copies(number, chip(distance)):
            start(copy)
    waited = []

    def ready(distance):
        number = order.index((distance + count) % count)
        if number not in waited:
            waited.append(number)
            for copy in core_copies(number, chip(distance)):
                copy.wait_recv()
        return chip(distance)

    streams = ((0, 0, 1, right, -1), (0, 2, 1, left, 1), (0, 1, 1, right, -1), (1, 0, 1, left, 1), (2, 0, 1, left, 1))

    def hop_on(hop):
        for way, (k, lo, blocks, device, sign) in enumerate(streams):
            c = ready(sign * (1 + hop))
            for i in range(blocks):
                total = parts[k][lo + i, c, core].astype(f32) + got[k][c, lo + i].astype(f32)
                if hop:
                    if i == 0:
                        slot = recv_refs[way].at[hop - 1]
                        remote(slot, slot, device, ring_send.at[way, hop - 1], ring_recv.at[way, hop - 1]).wait_recv()
                    total = total + recv_refs[way][hop - 1, i].astype(f32)
                if hop < count - 1:
                    send_refs[way][hop, i] = total.astype(bf16)
                else:
                    rows_refs[k][own, lo + i] = total.astype(bf16)
            if hop < count - 1:
                start(remote(send_refs[way].at[hop], recv_refs[way].at[hop], device, ring_send.at[way, hop], ring_recv.at[way, hop]))

    def swap():
        for d, t in enumerate(mates):
            start(remote(win_ref.at[t], win_out.at[team], {"team": t}, team_send.at[d], team_recv.at[d]))
            source = team + 3 - d - 4 * ((team + 3 - d) // 4)
            ends.append(remote(win_ref.at[t], win_out.at[source], {"team": t}, team_send.at[d], team_recv.at[d]))
        keep = pltpu.make_async_copy(win_ref.at[team], win_out.at[team], local_sem)
        keep.start()
        keeps.append(keep)

    keeps, here = [], []

    def have(*numbers):
        for k in numbers:
            if k not in here:
                here.append(k)
                bring[k].wait()

    mine, width = dx_ref.shape
    chunk = next(n for n in (512, 256, 128) if n_prompt % n == 0 and mine % n == 0)

    def front_rows(first):
        have(0, 1)
        return sum(
            nt(dqkv_ref[c, first : first + chunk, :], w_ref[:, c * width : (c + 1) * width]) for c in range(3)
        )

    def away_chunk(first):
        s, row = first // n_prompt, first % n_prompt
        away_ref[s, row : row + chunk, :] = front_rows(mine + first).astype(bf16)
        if row + chunk == n_prompt:
            start(remote(away_ref.at[s], home_ref.at[s], peers[s], away_send.at[s], away_recv.at[s]))

    def own_chunk(first):
        dx_ref[first : first + chunk, :] = front_rows(first)

    def last_chunk(first):
        have(2, 3)
        at = slice(first, first + chunk)
        x = x_ref[at, :].astype(f32)
        inverse = lax.rsqrt(jnp.mean(x * x, axis=-1, keepdims=True) + epsilon)
        unit = x * inverse
        dnormed = dx_ref[at, :]
        if first < n_prompt:
            for s in range(group - 1):
                dnormed = dnormed + home_ref[s, at, :].astype(f32)
        dunit = dnormed * gain_ref[0:1, :]
        dx_ref[at, :] = dmiddle_ref[at, :] + inverse * (dunit - unit * jnp.mean(dunit * unit, axis=-1, keepdims=True))

    fillers = [functools.partial(away_chunk, first) for first in range(0, (group - 1) * n_prompt, chunk)]
    fillers += [functools.partial(own_chunk, first) for first in range(0, mine, chunk)]

    def mix(unit):
        have(4, 5)
        mix_rows(unit, experts, padded, target_ref, gate_ref, middle_ref, back_ref, mixed_ref)

    fillers += [functools.partial(mix, unit) for unit in units]
    fillers += [functools.partial(last_chunk, first) for first in range(n_prompt, mine, chunk)]
    for hop in range(count - 1):
        hop_on(hop)
        if hop == 0:
            swap()
        for filler in fillers[hop * len(fillers) // (count - 1) : (hop + 1) * len(fillers) // (count - 1)]:
            filler()
    hop_on(count - 1)
    for s, peer in enumerate(peers):
        for k, rows in enumerate(rows_refs):
            start(remote(rows.at[own], rows.at[own], peer, row_send.at[k, s], row_recv.at[k, s]))
    for s in range(1, group):
        remote(away_ref.at[s - 1], home_ref.at[s - 1], peers[s - 1], away_send.at[s - 1], away_recv.at[s - 1]).wait_recv()
    for first in range(0, n_prompt, chunk):
        last_chunk(first)
    for s in range(1, group):
        other = lax.rem(own + group - s, group)
        for k, rows in enumerate(rows_refs):
            remote(rows.at[other], rows.at[other], peers[s - 1], row_send.at[k, s - 1], row_recv.at[k, s - 1]).wait_recv()
    for out, rows in zip(outs, rows_refs):
        for i in range(rows.shape[1]):
            total = rows[0, i].astype(f32)
            for j in range(1, group):
                total = total + rows[j, i].astype(f32)
            out[:, i * rows.shape[3] : (i + 1) * rows.shape[3]] = total
    for copy in ends:
        copy.wait_recv()
    for copy in started:
        copy.wait_send()
    for copy in keeps:
        copy.wait()


def finish(parts, grad_in, gain, target, gates, dqkv, w_qkv, x, dmiddle, middle, back, n_prompt, units, padded, cycle, group):
    count = len(cycle)
    depth = parts[0].shape[1]
    rows = depth // (2 * count)
    mine, width = dmiddle.shape
    experts = back.shape[0]
    shapes = [(v.shape[0], v.shape[2]) for v in parts]
    streams = [(1, shapes[0][1])] * 3 + [shapes[1], shapes[2]]
    anywhere, vmem = pl.BlockSpec(memory_space=pl.ANY), pl.BlockSpec(memory_space=pltpu.VMEM)
    ring = [pltpu.VMEM((count - 1, k, rows, n), bf16) for k, n in streams]
    return pl.pallas_call(
        functools.partial(finish_kernel, cycle, group, n_prompt, units, experts, padded),
        out_shape=tuple(jax.ShapeDtypeStruct((rows, k * n), f32) for k, n in shapes)
        + (
            jax.ShapeDtypeStruct(grad_in.shape, bf16),
            jax.ShapeDtypeStruct((mine, width), f32),
            jax.ShapeDtypeStruct((mine, width), bf16),
        ),
        in_specs=[vmem] * 3 + [anywhere] + [vmem] * 3 + [anywhere] * 6,
        out_specs=(vmem,) * 3 + (anywhere,) + (vmem,) * 2,
        scratch_shapes=[pltpu.VMEM((count, k, rows, n), bf16) for k, n in shapes]
        + ring
        + ring
        + [pltpu.VMEM((group, k, rows, n), bf16) for k, n in shapes]
        + [pltpu.VMEM((group - 1, n_prompt, width), bf16)] * 2
        + [
            pltpu.VMEM(dqkv.shape, bf16),
            pltpu.VMEM((depth, 3 * width), bf16),
            pltpu.VMEM((mine, width), bf16),
            pltpu.VMEM((mine, width), f32),
            pltpu.VMEM((mine, width), f32),
            pltpu.VMEM(back.shape, bf16),
        ]
        + [pltpu.SemaphoreType.DMA((3, count))] * 2
        + [pltpu.SemaphoreType.DMA((5, count))] * 2
        + [pltpu.SemaphoreType.DMA((3, group))] * 2
        + [pltpu.SemaphoreType.DMA((3,))] * 2
        + [pltpu.SemaphoreType.DMA((group,))] * 2
        + [pltpu.SemaphoreType.DMA, pltpu.SemaphoreType.DMA((6,))],
        compiler_params=pltpu.CompilerParams(collective_id=3, has_side_effects=True, vmem_limit_bytes=VMEM_LIMIT),
        cost_estimate=pl.CostEstimate(flops=3 * 10**10, bytes_accessed=10**8, transcendentals=0),
        name="finish",
    )(
        *[v.reshape(v.shape[0], count, 2, rows, v.shape[2]) for v in parts],
        grad_in,
        gain,
        target,
        gates,
        dqkv,
        w_qkv,
        x,
        dmiddle,
        middle,
        back,
    )


def scatter_expert(grad):
    return lax.psum_scatter(grad, "depth", scatter_dimension=0, tiled=True).reshape(4, -1, grad.shape[1])


def whole_kernel(kernel, out_shape, flops, name, *args):
    return pl.pallas_call(
        kernel,
        out_shape=out_shape,
        compiler_params=pltpu.CompilerParams(vmem_limit_bytes=VMEM_LIMIT),
        cost_estimate=pl.CostEstimate(flops=flops, bytes_accessed=sum(a.size * a.dtype.itemsize for a in args), transcendentals=0),
        name=name,
    )(*args)


def gelu_parts(x):
    a = 0.7978845608028654
    square = x * x
    t = jnp.tanh(x * (a + (a * 0.044715) * square))
    half = 0.5 + 0.5 * t
    return x * half, half + (0.5 * x) * (1.0 - t * t) * (a + (3 * a * 0.044715) * square)


def rms_inverse(x):
    return lax.rsqrt(jnp.mean(x * x, axis=-1, keepdims=True) + epsilon)


def rms_grad(x, inverse, gain, dnormed):
    unit = x * inverse
    dunit = dnormed * gain
    dx = inverse * (dunit - unit * jnp.mean(dunit * unit, axis=-1, keepdims=True))
    return dx, jnp.sum(dnormed * unit, axis=0)


def per_device(
    cycle,
    prompt_in,
    cont_in,
    prompt_cot,
    cont_cot,
    prompt_route,
    cont_route,
    rel_bucket,
    norm_attn,
    norm_ffn,
    w_qkv,
    w_out,
    rel_w,
    w_router,
    expert_in,
    expert_out,
):
    shard = w_qkv.shape[0]
    fsdp = lax.axis_size("depth") * lax.axis_size("team")
    group = lax.axis_size("expert")
    width = shard * fsdp
    head_count = rel_w.shape[1]
    head_size = width // head_count
    pairs = head_count // 2
    experts = w_router.shape[1]
    n_prompt, n_cont = prompt_in.shape[1], cont_in.shape[2]
    mine, prompt_len = n_prompt + n_cont, n_prompt * group
    cap_prompt = (10 * n_prompt + 4 * experts - 1) // (4 * experts)
    cap_cont = (10 * n_cont + 4 * experts - 1) // (4 * experts)
    padded = (cap_prompt + cap_cont + 15) // 16 * 16
    units = unit_list(n_prompt, n_cont, cap_prompt, cap_cont, padded)
    own = lax.axis_index("expert")
    own_list = jnp.reshape(own, (1,)).astype(jnp.int32)

    rel_rows = rel_w.shape[0] * head_count
    extra = [
        w_router,
        norm_attn[:, None],
        norm_ffn[:, None],
        jnp.pad(rel_w.reshape(-1), (0, shard - rel_rows))[:, None],
        jnp.zeros((shard, 128 - experts - 3), bf16),
    ]
    routes = jnp.concatenate([prompt_route[0], cont_route[0, 0]]).T
    routes = jnp.pad(routes, ((0, 6), (0, 0)), constant_values=-1)
    fixed = (units, ((n_prompt, cap_prompt), (n_cont, cap_cont)), experts, padded)
    qkv_full, out_full, misc, w_in, w_down, x_other, target, cot_slots = front(
        w_qkv, w_out, jnp.concatenate(extra, axis=1), expert_in, expert_out, prompt_in[0], routes, prompt_cot[0], cont_cot[0, 0], fixed, cycle, group
    )
    w_in = lax.all_gather(w_in.reshape(-1, w_in.shape[2]), "depth", axis=0, tiled=True)
    w_down = lax.all_gather(w_down.reshape(-1, w_down.shape[2]), "depth", axis=0, tiled=True)
    cots = lax.all_to_all(cot_slots, ("expert", "team"), split_axis=0, concat_axis=0, tiled=True)
    cot = jnp.concatenate([prompt_cot[0], cont_cot[0, 0]]).astype(f32)
    router_full = misc[:, :experts]
    gain_attn = misc[:, experts].astype(f32)
    gain_ffn = misc[:, experts + 1].astype(f32)
    rel_full = misc[:, experts + 2].reshape(fsdp, shard)[:, :rel_rows].reshape(-1, head_count)
    buckets = rel_full.shape[0]

    x_low = jnp.concatenate([prompt_in[0], cont_in[0, 0], x_other.reshape(-1, width)])
    x_all = x_low.astype(f32)
    x = x_all[:mine]
    bucket_hot = (rel_bucket[None, :] == jnp.arange(buckets, dtype=jnp.int32)[:, None]).astype(f32)
    dist_table = jnp.einsum("bt,bh->ht", bucket_hot, rel_full.astype(f32), precision=lax.Precision.HIGHEST)
    table = jnp.concatenate([jnp.full((head_count, prompt_len), blocked, f32), dist_table], axis=1)
    table = table.reshape(pairs, 2, -1)
    inverse_x = rms_inverse(x_all)
    normed = (x_all * inverse_x * gain_attn).astype(bf16)
    qkv = jnp.dot(normed, qkv_full, preferred_element_type=f32).astype(bf16)
    heads_out, lse = attend(own_list, table, qkv, n_prompt, n_cont, group, head_size)
    cots, heads_out = lax.optimization_barrier((cots, heads_out))

    middle = x + jnp.dot(heads_out, out_full, preferred_element_type=f32)
    inverse_m = rms_inverse(middle)
    normed_ffn = (middle * inverse_m * gain_ffn).astype(bf16)
    logits = lax.dot_general(router_full, normed_ffn, (((0,), (1,)), ((), ())), preferred_element_type=f32)
    hot = [(jnp.arange(experts, dtype=jnp.int32)[:, None] == routes[c : c + 1]).astype(f32) for c in range(2)]
    picked = jnp.stack([jnp.sum(logits * h, axis=0) for h in hot])
    gates = jax.nn.softmax(picked, axis=0)
    gate_rows = jnp.pad(gates, ((0, 6), (0, 0)))

    active, slope, grad_down, dproduced, arrived_t = expert_up(
        target, gate_rows, routes, normed_ffn, cots, w_in, units, group, experts, padded
    )
    sum_down = scatter_expert(grad_down)
    grad_in, dnormed, inner = expert_back(target, dproduced, slope, active, arrived_t, w_in, w_down, units, group, experts, padded)
    sum_in = scatter_expert(grad_in)
    active, inner = lax.optimization_barrier((active, inner))
    dpicked = inner[:2] - gates * jnp.sum(inner[:2], axis=0, keepdims=True)
    dlogits = hot[0] * dpicked[0] + hot[1] * dpicked[1]
    terms, left = [], dlogits
    for _ in range(3):
        terms.append(left.astype(bf16))
        left = left - terms[-1].astype(f32)
    terms = jnp.concatenate(terms)
    dnormed = dnormed + lax.dot_general(
        terms, jnp.concatenate([router_full] * 3, axis=1), (((0,), (1,)), ((), ())), preferred_element_type=f32
    )
    grad_router = lax.dot_general(normed_ffn, terms, (((0,), (1,)), ((), ())), preferred_element_type=f32)
    grad_router = jnp.sum(grad_router.reshape(width, 3, experts), axis=1)
    dmiddle_part, grad_gain_ffn = rms_grad(middle, inverse_m, gain_ffn, dnormed)
    dmiddle = cot + dmiddle_part
    dattn = dmiddle.astype(bf16)
    grad_out = lax.dot_general(heads_out, dattn, (((0,), (0,)), ((), ())), preferred_element_type=f32)
    dheads = lax.dot_general(dattn, out_full, (((1,), (1,)), ((), ())), preferred_element_type=f32).astype(bf16)

    produced = jnp.dot(active.reshape(-1, active.shape[2]), w_down, preferred_element_type=f32)
    produced = produced.astype(bf16).reshape(-1, padded, width)
    back = lax.all_to_all(produced, ("expert", "team"), split_axis=0, concat_axis=0, tiled=True)
    dheads, sum_down = lax.optimization_barrier((dheads, sum_down))
    sum_down = lax.all_to_all(sum_down, "team", split_axis=0, concat_axis=0, tiled=True)

    dqkv, drel = attend_grad(own_list, table, qkv, heads_out, dheads, lse, n_prompt, n_cont, group, head_size)
    grad_qkv = jnp.einsum("rd,cre->cde", normed, dqkv, preferred_element_type=f32).astype(bf16)
    drel = drel.reshape(head_count, -1)[:, prompt_len:]
    grad_rel = jnp.einsum("bt,ht->bh", bucket_hot, drel, precision=lax.Precision.HIGHEST)

    rel_column = jnp.pad(grad_rel.reshape(fsdp, rel_rows), ((0, 0), (0, shard - rel_rows))).reshape(width, 1)
    small = [grad_router, grad_gain_ffn[:, None], rel_column, jnp.zeros((width, 128 - experts - 2), f32)]
    small = jnp.concatenate(small, axis=1).astype(bf16)
    small, sum_down = lax.optimization_barrier((small, sum_down))
    sum_qkv, sum_out, small, sum_in, dx, mixed_out = finish(
        (grad_qkv, grad_out.astype(bf16)[None], small[None]),
        sum_in,
        jnp.broadcast_to(gain_attn[None], (8, width)),
        target,
        gate_rows,
        dqkv,
        qkv_full,
        x_low,
        dmiddle,
        middle,
        back,
        n_prompt,
        units,
        padded,
        cycle,
        group,
    )
    return (
        mixed_out[:n_prompt][None],
        mixed_out[n_prompt:][None, None],
        dx[:n_prompt][None],
        dx[n_prompt:][None, None],
        jnp.sum(sum_qkv * w_qkv.astype(f32), axis=1) / norm_attn.astype(f32),
        small[:, experts],
        sum_qkv,
        sum_out,
        small[:rel_rows, experts + 1].reshape(-1, head_count),
        small[:, :experts],
        sum_in.astype(f32),
        sum_down.astype(f32),
    )


def ring_of_chips(mesh):
    devices = mesh.devices[:, 0]
    chips = len(devices) // 2
    across = [getattr(d, "coords", None) for d in devices[::2]]
    if any(c is None for c in across):
        return list(range(chips))
    columns = len({tuple(c)[0] for c in across})
    levels = chips // columns
    if columns < 2 or levels % 2 or levels * columns != chips:
        return list(range(chips))
    cycle = [0]
    for z in range(levels):
        row = list(range(1, columns))
        cycle += [z * columns + i for i in (row if z % 2 == 0 else row[::-1])]
    return cycle + [z * columns for z in range(levels - 1, 0, -1)]


def solution(mesh):
    fsdp, group = mesh.devices.shape
    cycle = ring_of_chips(mesh)
    mesh = jax.sharding.Mesh(mesh.devices.reshape(fsdp // 4, 4, group), ("depth", "team", "expert"))
    rows = ("depth", "team")
    in_specs = (
        P(rows, "expert", None),
        P(rows, "expert", None, None),
        P(rows, "expert", None),
        P(rows, "expert", None, None),
        P(rows, "expert", None),
        P(rows, "expert", None, None),
        P(),
        P(rows),
        P(rows),
        P(rows, None),
        P(rows, None),
        P(rows, None),
        P(rows, None),
        P("expert", rows, None),
        P("expert", rows, None),
    )
    out_specs = (
        P(rows, "expert", None),
        P(rows, "expert", None, None),
        P(rows, "expert", None),
        P(rows, "expert", None, None),
        P(rows),
        P(rows),
        P(rows, None),
        P(rows, None),
        P(rows, None),
        P(rows, None),
        P("expert", rows, None),
        P("expert", rows, None),
    )
    return jax.shard_map(
        functools.partial(per_device, cycle),
        mesh=mesh,
        in_specs=in_specs,
        out_specs=out_specs,
        check_vma=False,
    )
```
